128 devices in a mesh: patch: 64 (over x_lo, y, z, core), chan: 2 (over x_hi).
Axes of the slice: x: 4 (x_hi: 2, x_lo: 2; x = x_hi * 2 + x_lo), y: 4, z: 4, core: 2. Of those that a mesh axis runs over, the one named last changes fastest.
Arguments:
- features: bfloat16 [64, 524288], P('chan', 'patch'), may hold values from -6 to 6
- offsets: int32 [8, 524288], P(None, 'patch'), may hold values from -513 to 513, as said below
- edge_weights: float32 [8, 524288], P(None, 'patch'), may hold values from -1 to 0
- mix: bfloat16 [8, 64, 64], P(None, None, 'chan'), may hold values from -0.25 to 0.25
- bias: float32 [64], P('chan'), may hold values from -3 to 3
- owners: int32 [2048, 1], P('patch'), may hold values from 0 to 63; in each aligned block of 32 rows (0 to 31, 32 to 63, ...) at most 2 rows name the same one
Outputs:
- coarse: bfloat16 [64, 64, 2, 4096], P('patch', None, None, 'chan')
The draws below stay inside these ranges and needn't reach their ends.
Inputs may be any that keep to these rules, and one draw needn't show every extreme that they name: `offsets`: A slot without a neighbour holds offset 0 and weight 0. `owners`: among the 32 blocks of one sub-patch no owner is named more than 2 times, a bound that some block reaches.
All inputs are finite; a program needn't handle non-finite values.
Results may differ from the reference program's by a relative error of at most 0.012.
Values may be sent and summed in bfloat16 or wider, within the bound.
A program may use at most 128 MiB of HBM per device.

```python
import math
import jax
import jax.numpy as jnp
import numpy as np
from jax import lax

C = 64
K = 8
NBR = 8
BLOCK = 256
STRIP = 2
HALO = 513
PIX = 524288
CG = 32
BLK_DEV = 32
BLOCKS = 2048
POOLED = 64
CAP = 2
N_PATCH = 64
N_CHAN = 2


def layout(key):
    side_len = math.isqrt(BLOCK)
    levels = side_len.bit_length() - 1
    pixel_ids = jnp.arange(PIX, dtype=jnp.int32)
    block_ids = pixel_ids // BLOCK
    inner = pixel_ids % BLOCK
    column = jnp.zeros_like(pixel_ids)
    row_pos = jnp.zeros_like(pixel_ids)
    for level in range(levels):
        column = column + inner // 4 ** level % 2 * 2 ** level
        row_pos = row_pos + inner // (2 * 4 ** level) % 2 * 2 ** level
    grid_x = block_ids % STRIP * side_len + column
    grid_y = block_ids // STRIP * side_len + row_pos
    height = PIX // BLOCK // STRIP * side_len
    breadth = STRIP * side_len
    observed = jax.random.randint(key, (PIX,), 0, 10, dtype=jnp.int32) > 0
    observed = observed | (pixel_ids < (STRIP + 2) * BLOCK)
    directions = [(1, 0), (-1, 0), (0, 1), (0, -1), (1, 1), (-1, -1), (1, -1), (-1, 1)]
    shifts = []
    usable_all = []
    targets = []
    for step_x, step_y in directions:
        near_x = grid_x + step_x
        near_y = grid_y + step_y
        inside = (near_x >= 0) & (near_x < breadth) & (near_y >= 0) & (near_y < height)
        clip_x = jnp.clip(near_x, 0, breadth - 1)
        clip_y = jnp.clip(near_y, 0, height - 1)
        near_blk = clip_y // side_len * STRIP + clip_x // side_len
        local_x = clip_x % side_len
        local_y = clip_y % side_len
        near_idx = jnp.zeros_like(pixel_ids)
        for level in range(levels):
            near_idx = near_idx + local_x // 2 ** level % 2 * 4 ** level
            near_idx = near_idx + local_y // 2 ** level % 2 * (2 * 4 ** level)
        near_pix = near_blk * BLOCK + near_idx
        usable = inside & observed & observed[near_pix]
        shifts.append(jnp.where(usable, near_pix - pixel_ids, 0))
        usable_all.append(usable)
        targets.append(jnp.where(usable, near_pix, pixel_ids))
    return (jnp.stack(shifts), jnp.stack(usable_all), jnp.stack(targets))


def draw_offsets(key, part):
    shifts, usable, targets = layout(key)
    return shifts.astype(jnp.int32)


def draw_edge_weights(key, part):
    shifts, usable, targets = layout(key)
    key = jax.random.fold_in(key, 23)
    rough = jnp.exp(jax.random.uniform(key, (PIX,), jnp.float32, -0.6931, 0.6931))
    factor = jnp.array([1.0, 1.0, 1.0, 1.0, 0.5, 0.5, 0.5, 0.5], jnp.float32)[:, None]
    strength = jnp.where(usable, factor * jnp.sqrt(rough[None, :] * rough[targets]), 0.0)
    degree = 1.0 + jnp.sum(strength, axis=0)
    return (-strength / jnp.sqrt(degree[None, :] * degree[targets])).astype(jnp.float32)


def shard_levels(own_key, dims, shards, low, top_value):
    def one(dim, parts):
        steps = jax.random.uniform(jax.random.fold_in(jax.random.fold_in(own_key, 6), dim), (parts,), jnp.float32, low / len(shards), top_value / len(shards))
        return jnp.repeat(jnp.exp(steps), dims[dim] // parts).reshape((-1,) + (1,) * (len(dims) - dim - 1))

    gain = one(*shards[0])
    for cut in shards[1:]:
        gain = gain * one(*cut)
    return gain


def assign_block(own_key, own, number, rows, amount, top, bound, lean):
    sequence = jax.random.permutation(own_key, amount)
    crowded, usual = load_shares(amount, rows * top, bound, lean, True), load_shares(amount, rows * top, bound, lean, False)
    places = jnp.arange(amount)

    def named(sizes, turn):
        used = int((sizes > 0).sum())
        fixed = max(1, used // 4)
        passed = fixed + (places - fixed + turn * (used - fixed)) % max(1, amount - fixed)
        return jnp.zeros((amount,), jnp.int32).at[sequence[jnp.where(places < fixed, places, passed)]].set(jnp.asarray(sizes, jnp.int32))

    sizes = jnp.where(number % 4 == 0, named(crowded, number // 4), named(usual, number - number // 4 - 1))
    mixed = jax.random.permutation(jax.random.fold_in(own, 3), amount)
    source_of, receiver = mixed[0:amount // 2 * 2:2], mixed[1:amount // 2 * 2:2]
    room = jnp.minimum(sizes[source_of] - 1, bound - sizes[receiver]) // 2
    room = jnp.where((source_of == sequence[0]) | (receiver == sequence[0]) | (sizes[receiver] == 0), 0, jnp.maximum(room, 0))
    passed = jax.random.randint(jax.random.fold_in(own, 4), (amount // 2,), 0, 1 << 20) % (room + 1)
    sizes = sizes.at[source_of].add(-passed).at[receiver].add(passed)
    items = jnp.searchsorted(jnp.cumsum(sizes), jnp.arange(rows * top), side="right").astype(jnp.int32)
    grid = items.reshape(top, rows).T
    grid = grid[jax.random.permutation(jax.random.fold_in(own, 1), rows)]
    turn = jax.random.randint(jax.random.fold_in(own, 2), (rows, 1), 0, top)
    return jnp.take_along_axis(grid, (jnp.arange(top)[None, :] + turn) % top, axis=1)


def load_shares(amount, total, reach, skew, full):
    weights = [(1 << 20) // math.isqrt(rank ** skew) + 1 for rank in range(1, amount + 1)]
    largest = reach if full else min(reach, max(-(-total // amount), total * weights[0] // sum(weights)))
    least = 1 if total - largest >= amount - 1 else 0
    given, rest = [largest] + [least] * (amount - 1), total - largest - least * (amount - 1)
    while rest > 0:
        candidates = [i for i in range(1, amount) if given[i] < largest] or [i for i in range(1, amount) if given[i] < reach]
        whole, budget = sum([weights[i] for i in candidates]), rest
        for i in candidates:
            more = min(reach - given[i], max(1, budget * weights[i] // whole), rest)
            given[i] = given[i] + more
            rest = rest - more
    return np.array(given)


def normal_values(key, extent, deviation, limit, shards=(), kind=jnp.bfloat16):
    result = jax.random.normal(key, extent, jnp.float32) * deviation
    if len(shards) > 0:
        result = shard_levels(key, extent, shards, -0.22, 0.18) * result
    return jnp.clip(result, min=-limit, max=limit).astype(kind)


def setup_inputs(seed: int = 0) -> dict:
    key_list = jax.random.split(jax.random.key(seed), 7)
    features = normal_values(key_list[0], (C, PIX), 1.0, 6.0, ((0, 2), (1, 64)))
    offsets = draw_offsets(jax.random.fold_in(key_list[6], 71), 0)
    edge_weights = draw_edge_weights(jax.random.fold_in(key_list[6], 71), 0)
    mix = normal_values(key_list[3], (K, C, C), (K * C) ** -0.5, 0.25, ((2, 2),))
    bias = normal_values(key_list[4], (C,), 0.5, 3.0, ((0, 2),), jnp.float32)
    owners_keys = jax.random.split(jax.random.fold_in(key_list[5], 1), BLOCKS // BLK_DEV)
    owners_turns = jax.random.permutation(jax.random.fold_in(key_list[5], 3), BLOCKS // BLK_DEV)
    owners = jax.vmap(lambda own, number: assign_block(jax.random.fold_in(key_list[5], 2), own, number, BLK_DEV, N_PATCH, 1, CAP, 2))(owners_keys, owners_turns).reshape((BLOCKS, 1))
    return dict(features=features, offsets=offsets, edge_weights=edge_weights, mix=mix, bias=bias, owners=owners)


def neighbour_sum(values, offsets, edge_weights):
    padded = jnp.pad(values, ((HALO, HALO), (0, 0)))
    base = jnp.arange(values.shape[0], dtype=jnp.int32) + HALO
    total = jnp.zeros_like(values)
    for slot_index in range(NBR):
        picked = jnp.take(padded, base + offsets[slot_index], axis=0)
        total = total + edge_weights[slot_index][:, None] * picked
    return total


def chebyshev_mix(start, weights, offsets, edge_weights):
    acc = jnp.dot(start.astype(jnp.bfloat16), weights[0].T, preferred_element_type=jnp.float32)
    previous = start
    current = neighbour_sum(start, offsets, edge_weights)
    acc = acc + jnp.dot(current.astype(jnp.bfloat16), weights[1].T, preferred_element_type=jnp.float32)
    for term_index in range(2, K):
        following = 2.0 * neighbour_sum(current, offsets, edge_weights) - previous
        acc = acc + jnp.dot(following.astype(jnp.bfloat16), weights[term_index].T, preferred_element_type=jnp.float32)
        previous, current = current, following
    return acc


def reference(features, offsets, edge_weights, mix, bias, owners):
    width = math.gcd(16, CG)
    count = CG // width
    total = jnp.zeros((PIX, C), jnp.float32)
    for group in range(N_CHAN):
        half = features[group * CG:(group + 1) * CG].astype(jnp.float32)
        pieces = half.reshape(count, width, PIX).transpose(0, 2, 1)
        wpieces = mix[:, :, group * CG:(group + 1) * CG].reshape(K, C, count, width).transpose(2, 0, 1, 3)

        def advance(part, inputs):
            start, weights = inputs
            return part + chebyshev_mix(start, weights, offsets, edge_weights), None

        part, _ = lax.scan(advance, jnp.zeros((PIX, C), jnp.float32), (pieces, wpieces))
        rounded = lax.optimization_barrier(part.astype(jnp.bfloat16))
        total = total + rounded.astype(jnp.float32)
    filtered = jax.nn.relu(total + bias[None, :]).astype(jnp.bfloat16)
    pooled = filtered.astype(jnp.float32).reshape(PIX // 4, 4, C).mean(axis=1).astype(jnp.bfloat16)
    blocks = pooled.reshape(BLOCKS, POOLED, C).transpose(0, 2, 1).reshape(BLOCKS, C * POOLED)
    dest = owners[:, 0]
    onehot = (dest[:, None] == jnp.arange(N_PATCH, dtype=jnp.int32)[None, :]).astype(jnp.int32)
    grouped = onehot.reshape(N_PATCH, BLK_DEV, N_PATCH)
    ranks = jnp.cumsum(grouped, axis=1) - grouped
    slot = jnp.sum(ranks * grouped, axis=2).reshape(BLOCKS).astype(jnp.int32)
    source = (jnp.arange(BLOCKS, dtype=jnp.int32) // BLK_DEV).astype(jnp.int32)
    coarse = jnp.zeros((N_PATCH, N_PATCH, CAP, C * POOLED), jnp.bfloat16)
    return coarse.at[dest, source, slot].set(blocks)
```

```python
import functools

import jax
import jax.numpy as jnp
from jax import lax
from jax.experimental import pallas as pl
from jax.experimental.pallas import tpu as pltpu
from jax.sharding import PartitionSpec as P

MESH = pl.DeviceIdType.MESH
BF = jnp.bfloat16
F32 = jnp.float32
K = 8
CH = 64
OWN = 16
EXT = 7
NB = OWN + EXT
HALO = 640
LANES = HALO + NB * 256 + HALO
OUT_W = EXT * 256 + HALO
WIN = 1280
NPX = NB * 256
S3 = 1152
S4 = 1664


def place(line):
    n, q = line // 4, line % 4
    return 2 * n + q % 2, (q // 2 + n % 2) % 2


def iota(shape, dim):
    return lax.broadcasted_iota(jnp.int32, shape, dim)


def cheb_kernel(np_, feat, offs, wts, mix, bias, own_ref, out_ref,
                tb, fp, wm, ot, wt, cor, s16, w16, x3, mixall, biasall, inv, inv_s,
                msg, snd, t0_s, t0_r, tab_l, tab_s, tab_r, par_s, par_r,
                in_s, in_r, mid_s, mid_r, sw_s, sw_r, loc):
    p = lax.axis_index("patch")
    g = lax.axis_index("chan")
    n, c = p // 2, p % 2
    gx = (g + n) % 2
    line = 4 * n + 2 * gx + c
    last = 2 * np_ - 1
    sib = (p + 1 - 2 * c, g)
    partner = (p, 1 - g)
    first_core = c == 0
    home = gx == c
    ng = np_ // 2

    outer = pl.multiple_of((1 - c) * 0 + c * (LANES - OUT_W), 128)
    for k in range(1, K - 1):
        tb[k, :, pl.ds(outer, OUT_W)] = jnp.zeros((CH, OUT_W), BF)
    at_end = (line == 0) | (line == last)

    @pl.when(at_end)
    def _():
        tb[0, :, pl.ds(outer, OUT_W)] = jnp.zeros((CH, OUT_W), BF)
        to = pl.multiple_of(c * OWN * 256, 128)
        ot[:, pl.ds(to, EXT * 256)] = jnp.zeros((8, EXT * 256), jnp.int32)
        wt[:, pl.ds(to, EXT * 256)] = jnp.zeros((8, EXT * 256), F32)

    msg[2 * OWN] = jnp.zeros((16, 128), BF)

    bar = pltpu.get_barrier_semaphore()
    for dn in (-1, 0, 1):
        for dc in (0, 1):
            for dg in (0, 1):
                pp = 2 * (n + dn) + dc

                @pl.when((n + dn >= 0) & (n + dn < ng) & ~((pp == p) & (dg == g)))
                def _():
                    pl.semaphore_signal(bar, inc=1, device_id=(pp, dg), device_id_type=MESH)
    pl.semaphore_wait(bar, 11 - 4 * jnp.where((n == 0) | (n == ng - 1), 1, 0))

    half = 4096
    main_dst = pl.multiple_of((1 - c) * EXT * 256, 128)
    ext_dst = pl.multiple_of(c * OWN * 256, 128)
    sib_dst = pl.multiple_of(c * EXT * 256, 128)

    def tables(fn):
        fn(0, offs, ot)
        fn(1, wts, wt)

    def tab_main_local(i, src, dst):
        return pltpu.make_async_copy(src.at[:, pl.ds(pl.multiple_of(c * half, 128), half)],
                                     dst.at[:, pl.ds(main_dst, half)], tab_l.at[i])

    def tab_main_remote(i, src, dst):
        return pltpu.make_async_remote_copy(
            src_ref=src.at[:, pl.ds(pl.multiple_of((1 - c) * half, 128), half)],
            dst_ref=dst.at[:, pl.ds(sib_dst, half)],
            send_sem=tab_s.at[i], recv_sem=tab_r.at[i], device_id=sib, device_id_type=MESH)

    def tab_ext_local(i, src, dst):
        return pltpu.make_async_copy(
            src.at[:, pl.ds(pl.multiple_of((1 - c) * (8192 - EXT * 256), 128), EXT * 256)],
            dst.at[:, pl.ds(ext_dst, EXT * 256)], tab_l.at[i])

    out_line = line - 1 + 2 * c
    outp, outg = place(out_line)
    has_out = ~at_end
    other_ext = pl.multiple_of((1 - c) * OWN * 256, 128)

    def tab_ext_remote(i, src, dst):
        return pltpu.make_async_remote_copy(
            src_ref=src.at[:, pl.ds(pl.multiple_of(c * (8192 - EXT * 256), 128), EXT * 256)],
            dst_ref=dst.at[:, pl.ds(other_ext, EXT * 256)],
            send_sem=tab_s.at[2 + i], recv_sem=tab_r.at[2 + i],
            device_id=(outp, outg), device_id_type=MESH)

    @pl.when(home)
    def _():
        tables(lambda i, s, d: tab_main_local(i, s, d).start())
        tables(lambda i, s, d: tab_main_remote(i, s, d).start())

    @pl.when(~home)
    def _():
        tables(lambda i, s, d: tab_ext_local(i, s, d).start())

    row = pl.multiple_of(32 * g, 32)
    flows = (
        (2 * p, 0, HALO + 4096, LANES - HALO - 4096, 0),
        (2 * p + 1, 4096 - HALO, HALO + 4096, 0, 0),
        (2 * p - 1, 0, OUT_W, LANES - OUT_W, 2),
        (2 * p + 2, 8192 - OUT_W, OUT_W, 0, 2),
    )

    def flow_parts(i):
        target, src0, size, dst0, sem = flows[i]
        src = feat.at[:, pl.ds(src0, size)]
        dst = tb.at[0, pl.ds(row, 32), pl.ds(dst0, size)]
        return target, src, dst, sem + g

    def flow_ok(i):
        target = flows[i][0]
        return (target >= 0) & (target <= last)

    def flow_remote(i):
        target, src, dst, sem = flow_parts(i)
        tp, tg = place(target)
        return pltpu.make_async_remote_copy(
            src_ref=src, dst_ref=dst, send_sem=t0_s.at[i], recv_sem=t0_r.at[sem],
            device_id=(tp, tg), device_id_type=MESH)

    for i in range(4):
        target, src, dst, sem = flow_parts(i)

        @pl.when(flow_ok(i) & (target == line))
        def _():
            pltpu.make_async_copy(src, dst, t0_r.at[sem]).start()

        @pl.when(flow_ok(i) & (target != line))
        def _():
            flow_remote(i).start()

    @pl.when(home & has_out)
    def _():
        tables(lambda i, s, d: tab_ext_remote(i, s, d).start())

    mixcat = jnp.concatenate([mix[k] for k in range(K)], axis=0)
    oi, oo = iota((64, 64), 0), iota((64, 64), 1)
    wanted = (oi // 16 % 2) * 32 + 2 * (oi % 16) + oi // 32
    perm = jnp.where(oo == wanted, 1.0, 0.0).astype(BF)
    mixall[g] = lax.dot_general(perm, mixcat, (((1,), (1,)), ((), ())),
                                preferred_element_type=F32).astype(BF)
    biasall[g] = jnp.zeros((8, 128), F32)
    biasall[g, 0:1, 0:32] = bias[...]

    rowv = jnp.broadcast_to(own_ref[...], (32, 32))
    si, sl = iota((32, 32), 0), iota((32, 32), 1)
    bi, bl = iota((32, 128), 0), iota((32, 128), 1)
    col = jnp.sum(jnp.where(si == sl, rowv, 0), axis=1, keepdims=True)
    same = (jnp.broadcast_to(col, (32, 32)) == rowv) & (sl < si)
    slot = jnp.sum(jnp.where(same, 1, 0), axis=1, keepdims=True)
    key = col * 2 + slot
    hit = jnp.sum(jnp.where(jnp.broadcast_to(key, (32, 128)) == bl, bi + 1, 0), axis=0, keepdims=True)
    inv[c] = jnp.broadcast_to(jnp.where(hit == 0, 2 * OWN, hit - 1), (8, 128))

    par = [
        pltpu.make_async_remote_copy(src_ref=mixall.at[g], dst_ref=mixall.at[g], send_sem=par_s.at[0],
                                     recv_sem=par_r.at[0], device_id=partner, device_id_type=MESH),
        pltpu.make_async_remote_copy(src_ref=biasall.at[g], dst_ref=biasall.at[g], send_sem=par_s.at[1],
                                     recv_sem=par_r.at[1], device_id=partner, device_id_type=MESH),
        pltpu.make_async_remote_copy(src_ref=inv.at[c], dst_ref=inv.at[c], send_sem=par_s.at[2],
                                     recv_sem=par_r.at[2], device_id=sib, device_id_type=MESH),
    ]
    for cp in par:
        cp.start()

    def block_of(i):
        return c * i + (1 - c) * (NB - 1 - i)

    base = [(iota((16, 256), 0) + 16 * r).astype(jnp.int16) for r in range(16)]

    def build(i, carry):
        b = block_of(i)
        lanes = pl.ds(pl.multiple_of(256 * b, 256), 256)
        s = iota((8, 256), 1) + ot[:, lanes] + 512
        w = wt[:, lanes]
        cl = jnp.sum(jnp.where(s == -1, w, 0.0), axis=0, keepdims=True)
        cr = jnp.sum(jnp.where(s == WIN, w, 0.0), axis=0, keepdims=True)
        cor[b, 0:1, :] = cl
        cor[b, 1:2, :] = cr
        full = w
        for r in range(1, 8):
            full = full + jnp.where(s == pltpu.roll(s, r, 0), pltpu.roll(w, r, 0), 0.0)
        for j in range(8):
            s16[j] = jnp.broadcast_to(s[j:j + 1], (16, 256)).astype(jnp.int16)
            w16[j] = jnp.broadcast_to(full[j:j + 1], (16, 256)).astype(BF)
        for q in range(WIN // 256):
            acc = [jnp.zeros((16, 256), BF)] * 16
            for j in range(8):
                sq = s16[j] - jnp.int16(256 * q)
                wq = w16[j]
                acc = [jnp.where(base[r] == sq, wq, acc[r]) for r in range(16)]
            for r in range(16):
                wm[b, 256 * q + 16 * r:256 * q + 16 * (r + 1), :] = acc[r]
        return carry

    lo1 = jnp.where(home, 0, OWN)
    hi1 = jnp.where(home, OWN, NB)
    lo2 = jnp.where(home, OWN, 0)
    hi2 = jnp.where(home, NB, OWN)

    @pl.when(home)
    def _():
        tables(lambda i, s, d: tab_main_local(i, s, d).wait())

    @pl.when(~home)
    def _():
        tables(lambda i, s, d: tab_ext_local(i, s, d).wait())

    lax.fori_loop(lo1, hi1, build, 0)

    @pl.when(~home)
    def _():
        tables(lambda i, s, d: pltpu.make_async_copy(
            s.at[:, pl.ds(0, half)], d.at[:, pl.ds(main_dst, half)], tab_r.at[i]).wait())

    @pl.when(home & has_out)
    def _():
        tables(lambda i, s, d: pltpu.make_async_copy(
            s.at[:, pl.ds(0, EXT * 256)], d.at[:, pl.ds(ext_dst, EXT * 256)], tab_r.at[2 + i]).wait())

    lax.fori_loop(lo2, hi2, build, 0)

    main_at = pl.multiple_of((1 - c) * (LANES - HALO - 4096), 128)
    for gg in range(2):
        pltpu.make_async_copy(feat.at[:, pl.ds(0, HALO + 4096)],
                              tb.at[0, pl.ds(32 * gg, 32), pl.ds(main_at, HALO + 4096)],
                              t0_r.at[gg]).wait()

        @pl.when(has_out)
        def _():
            pltpu.make_async_copy(feat.at[:, pl.ds(0, OUT_W)],
                                  tb.at[0, pl.ds(32 * gg, 32), pl.ds(outer, OUT_W)],
                                  t0_r.at[2 + gg]).wait()

    def block(k, i):
        b = block_of(i)
        at = pl.multiple_of(256 * b, 256)
        win = tb[k - 1, :, pl.ds(at + 128, WIN)]
        u = jnp.dot(win, wm[b], preferred_element_type=F32)
        left = pltpu.roll(tb[k - 1, :, pl.ds(at, 128)].astype(F32), 1, 1)
        right = pltpu.roll(tb[k - 1, :, pl.ds(at + 1408, 128)].astype(F32), 127, 1)
        u = u + jnp.concatenate([left * cor[b, 0:1, 0:128], right * cor[b, 1:2, 128:256]], axis=1)
        if k == 1:
            t = u
        elif k == 2:
            t = 2.0 * u - tb[0, :, pl.ds(at + HALO, 256)].astype(F32)
        else:
            t = 2.0 * u - fp[k % 2, :, pl.ds(at, 256)]
        if k < K - 1:
            fp[k % 2, :, pl.ds(at, 256)] = t
        tb[k, :, pl.ds(at + HALO, 256)] = t.astype(BF)

    def run(k, lo, hi, group=4):
        full = (hi - lo) // group

        def some(m, carry):
            for r in range(group):
                block(k, lo + m * group + r)
            return carry

        if full > 1:
            lax.fori_loop(0, full, some, 0)
            lo = lo + full * group
        for i in range(lo, hi):
            block(k, i)

    own_at = HALO + (1 - c) * EXT * 256
    edge_src = pl.multiple_of(own_at + (1 - c) * (4096 - HALO), 128)
    edge_dst = pl.multiple_of(c * (LANES - HALO), 128)

    def inner(k):
        return pltpu.make_async_remote_copy(
            src_ref=tb.at[k, :, pl.ds(edge_src, HALO)], dst_ref=tb.at[k, :, pl.ds(edge_dst, HALO)],
            send_sem=in_s.at[k], recv_sem=in_r.at[k], device_id=sib, device_id_type=MESH)

    def outer_copy(k, width, m):
        src = pl.multiple_of(own_at + c * (4096 - width), 128)
        if k == 3:
            dst = x3.at[:, :]
        else:
            dst = tb.at[k, :, pl.ds(pl.multiple_of((1 - c) * (LANES - OUT_W) + c * (OUT_W - width), 128), width)]
        return pltpu.make_async_remote_copy(
            src_ref=tb.at[k, :, pl.ds(src, width)], dst_ref=dst,
            send_sem=mid_s.at[m], recv_sem=mid_r.at[m], device_id=(outp, outg), device_id_type=MESH)

    run(1, 0, 3)
    inner(1).start()
    run(1, 3, 23)
    inner(1).wait_recv()
    run(2, 0, 3)
    inner(2).start()
    run(2, 3, 21)
    inner(2).wait_recv()
    run(3, 0, 3)
    inner(3).start()
    run(3, 3, 19)

    @pl.when(has_out)
    def _():
        outer_copy(3, S3, 0).start()

    inner(3).wait_recv()
    run(4, 9, 16)

    @pl.when(has_out)
    def _():
        outer_copy(4, S4, 1).start()

    run(4, 0, 3)
    inner(4).start()
    run(4, 3, 9)
    inner(4).wait_recv()
    run(5, 0, 3)
    inner(5).start()
    run(5, 3, 13)

    @pl.when(has_out)
    def _():
        outer_copy(3, S3, 0).wait_recv()
        outer_copy(4, S4, 1).wait_recv()
        d3 = pl.multiple_of((1 - c) * (EXT * 256 - S3) + c * OWN * 256, 128)
        fp[1, :, pl.ds(d3, S3)] = x3[...].astype(F32)
        d4 = pl.multiple_of((1 - c) * (EXT * 256 - 768) + c * OWN * 256, 128)
        fp[0, :, pl.ds(d4, 768)] = tb[4, :, pl.ds(d4 + HALO, 768)].astype(F32)

    run(5, 13, 21)
    inner(5).wait_recv()
    run(6, 0, 3)
    inner(6).start()
    run(6, 3, 19)
    inner(6).wait_recv()
    run(7, 0, 16)

    pltpu.make_async_copy(mixall.at[1 - g], mixall.at[1 - g], par_r.at[0]).wait()
    pltpu.make_async_copy(biasall.at[1 - g], biasall.at[1 - g], par_r.at[1]).wait()
    pltpu.make_async_copy(inv.at[1 - c], inv.at[1 - c], par_r.at[2]).wait()
    to_smem = pltpu.make_async_copy(inv.at[gx], inv_s, loc.at[0])
    to_smem.start()
    o1, l1 = iota((64, 128), 0), iota((64, 128), 1)
    brow = jnp.where(o1 // 16 % 2 == 0, biasall[0, 0:1, :], biasall[1, 0:1, :])
    bcol = jnp.sum(jnp.where(l1 == 2 * (o1 % 16) + o1 // 32, brow, 0.0), axis=1, keepdims=True)
    pi, pq = iota((512, 128), 0), iota((512, 128), 1)
    pool = jnp.where(pi % 256 // 4 + 64 * (pi // 256) == pq, 0.25, 0.0).astype(BF)

    def finish(b, carry):
        at = pl.multiple_of(own_at + 256 * b, 128)
        total = bcol
        for gg in range(2):
            rhs = jnp.concatenate([tb[k, 32 * gg:32 * gg + 32, pl.ds(at, 256)] for k in range(K)], axis=0)
            part = jnp.dot(mixall[gg], rhs, preferred_element_type=F32)
            total = total + part.astype(BF).astype(F32)
        filt = jnp.maximum(total, 0.0).astype(BF)
        lhs = jnp.concatenate([filt[0:32], filt[32:64]], axis=1)
        pooled = jnp.dot(lhs, pool, preferred_element_type=F32).astype(BF)
        sel = jnp.where(c == 0, pooled[0:16].astype(F32), pooled[16:32].astype(F32)).astype(BF)
        oth = jnp.where(c == 0, pooled[16:32].astype(F32), pooled[0:16].astype(F32)).astype(BF)
        msg[c * OWN + b] = sel
        snd[b] = oth
        return carry

    def swap(m):
        part = pl.ds(pl.multiple_of(8 * m, 8), 8)
        return pltpu.make_async_remote_copy(
            src_ref=snd.at[part], dst_ref=msg.at[pl.ds(c * OWN + 8 * m, 8)],
            send_sem=sw_s.at[m], recv_sem=sw_r.at[m], device_id=sib, device_id_type=MESH)

    for m in range(2):
        for r in range(8):
            finish(8 * m + r, 0)
        swap(m).start()
    to_smem.wait()
    for m in range(2):
        pltpu.make_async_copy(msg.at[pl.ds((1 - c) * OWN + 8 * m, 8)],
                              msg.at[pl.ds((1 - c) * OWN + 8 * m, 8)], sw_r.at[m]).wait()

    ei, ej = iota((32, 32), 0), iota((32, 32), 1)
    weave = jnp.where(ej == (ei % 2) * 16 + ei // 2, 1.0, 0.0).astype(BF)

    def assemble(m, carry):
        cols = []
        for r in range(4):
            o = 4 * m + r
            cols.append(jnp.concatenate([msg[inv_s[0, 2 * o]], msg[inv_s[0, 2 * o + 1]]], axis=0))
        res = jnp.dot(weave, jnp.concatenate(cols, axis=1), preferred_element_type=F32).astype(BF)
        for r in range(4):
            out_ref[4 * m + r] = res[:, 128 * r:128 * (r + 1)]
        return carry

    lax.fori_loop(0, np_ // 4, assemble, 0)

    @pl.when(home)
    def _():
        tables(lambda i, s, d: tab_main_remote(i, s, d).wait_send())

    @pl.when(home & has_out)
    def _():
        tables(lambda i, s, d: tab_ext_remote(i, s, d).wait_send())

    for i in range(4):
        @pl.when(flow_ok(i) & (flows[i][0] != line))
        def _():
            flow_remote(i).wait_send()

    for cp in par:
        cp.wait_send()
    for k in range(1, K - 1):
        inner(k).wait_send()

    @pl.when(has_out)
    def _():
        outer_copy(3, S3, 0).wait_send()
        outer_copy(4, S4, 1).wait_send()

    for m in range(2):
        swap(m).wait_send()


def dispatch_kernel(np_, out_ref, got_ref, ss, rs):
    p = lax.axis_index("patch")
    g = lax.axis_index("chan")
    n, c = p // 2, p % 2
    src = 2 * n + (g + n) % 2
    bar = pltpu.get_barrier_semaphore()

    def hello(i, carry):
        j = (i + p) % np_
        pp = 2 * (j // 2) + g
        gg = j % 2

        @pl.when(~((pp == p) & (gg == g)))
        def _():
            pl.semaphore_signal(bar, inc=1, device_id=(pp, gg), device_id_type=MESH)
        return carry

    lax.fori_loop(0, np_, hello, 0)
    pl.semaphore_wait(bar, np_ - jnp.where(c == g, 1, 0))

    def copy(o):
        return pltpu.make_async_remote_copy(
            src_ref=out_ref.at[o], dst_ref=got_ref.at[src], send_sem=ss.at[o], recv_sem=rs.at[src],
            device_id=(o, c), device_id_type=MESH)

    def send(i, carry):
        o = (p + i) % np_
        me = (o == p) & (c == g)

        @pl.when(me)
        def _():
            pltpu.make_async_copy(out_ref.at[o], got_ref.at[src], rs.at[src]).start()

        @pl.when(~me)
        def _():
            copy(o).start()
        return carry

    lax.fori_loop(0, np_, send, 0)

    def take(i, carry):
        pltpu.make_async_copy(got_ref.at[i], got_ref.at[i], rs.at[i]).wait()
        return carry

    lax.fori_loop(0, np_, take, 0)

    def sent(o, carry):
        @pl.when(~((o == p) & (c == g)))
        def _():
            copy(o).wait_send()
        return carry

    lax.fori_loop(0, np_, sent, 0)


def body(features, offsets, edge_weights, mix, bias, owners):
    np_ = lax.axis_size("patch")
    any_, vmem = pl.BlockSpec(memory_space=pl.ANY), pl.BlockSpec(memory_space=pltpu.VMEM)
    dma, vm = pltpu.SemaphoreType.DMA, pltpu.VMEM
    out = pl.pallas_call(
        functools.partial(cheb_kernel, np_),
        out_shape=jax.ShapeDtypeStruct((np_, 32, 128), BF),
        in_specs=[any_, any_, any_, vmem, vmem, vmem],
        out_specs=vmem,
        scratch_shapes=[
            vm((K, CH, LANES), BF), vm((2, CH, NPX), F32), vm((NB, WIN, 256), BF),
            vm((8, NPX), jnp.int32), vm((8, NPX), F32), vm((NB, 8, 256), F32),
            vm((8, 16, 256), jnp.int16), vm((8, 16, 256), BF), vm((CH, S3), BF),
            vm((2, 64, 256), BF), vm((2, 8, 128), F32), vm((2, 8, 128), jnp.int32),
            pltpu.SMEM((8, 128), jnp.int32),
            vm((2 * OWN + 1, 16, 128), BF), vm((OWN, 16, 128), BF),
            dma((4,)), dma((4,)), dma((2,)), dma((4,)), dma((4,)), dma((3,)), dma((3,)),
            dma((K,)), dma((K,)), dma((2,)), dma((2,)), dma((2,)), dma((2,)), dma((1,)),
        ],
        compiler_params=pltpu.CompilerParams(
            vmem_limit_bytes=62 << 20, collective_id=0, has_side_effects=True),
        name="cheb",
    )(features, offsets, edge_weights, mix.transpose(0, 2, 1), bias.reshape(1, -1), owners.reshape(1, -1))
    got = pl.pallas_call(
        functools.partial(dispatch_kernel, np_),
        out_shape=jax.ShapeDtypeStruct((np_, 32, 128), BF),
        in_specs=[any_],
        out_specs=any_,
        scratch_shapes=[dma((np_,)), dma((np_,))],
        compiler_params=pltpu.CompilerParams(
            vmem_limit_bytes=62 << 20, collective_id=1, has_side_effects=True),
        name="dispatch",
    )(out)
    got = got.reshape(np_, 16, 2, 128).transpose(0, 2, 1, 3).reshape(np_, 2, 2048)
    return got[None]


def solution(mesh):
    return jax.shard_map(
        body,
        mesh=mesh,
        in_specs=(
            P("chan", "patch"),
            P(None, "patch"),
            P(None, "patch"),
            P(None, None, "chan"),
            P("chan"),
            P("patch", None),
        ),
        out_specs=P("patch", None, None, "chan"),
        check_vma=False,
    )
```

```python
import functools

import jax
import jax.numpy as jnp
from jax import lax
from jax.experimental import pallas as pl
from jax.experimental.pallas import tpu as pltpu
from jax.sharding import PartitionSpec as P

MESH = pl.DeviceIdType.MESH
BF = jnp.bfloat16
F32 = jnp.float32
K = 8
CH = 64
OWN = 16
EXT = 7
NB = OWN + EXT
HALO = 640
LANES = HALO + NB * 256 + HALO
OUT_W = EXT * 256 + HALO
WIN = 1280
NPX = NB * 256
S3 = 1152
S4 = 1664


def place(line):
    n, q = line // 4, line % 4
    return 2 * n + q % 2, (q // 2 + n % 2) % 2


def iota(shape, dim):
    return lax.broadcasted_iota(jnp.int32, shape, dim)


def cheb_kernel(np_, feat, offs, wts, mix, bias, own_ref, out_ref,
                tb0, tb1, tb2, tb3, tb4, tb5, tb6, fp0, fp1,
                wm, ot, wt, cor, s16, w16, x3, mixall, biasall, inv, inv_s,
                msg, snd, outg, t0_s, t0_r, tab_l, tab_s, tab_r, par_s, par_r,
                in_s, in_r, mid_s, mid_r, sw_s, sw_r, loc, all_s, all_r):
    tb = (tb0, tb1, tb2, tb3, tb4, tb5, tb6)
    fp = (fp0, fp1)
    p = lax.axis_index("patch")
    g = lax.axis_index("chan")
    n, c = p // 2, p % 2
    gx = (g + n) % 2
    line = 4 * n + 2 * gx + c
    last = 2 * np_ - 1
    sib = (p + 1 - 2 * c, g)
    partner = (p, 1 - g)
    first_core = c == 0
    home = gx == c
    ng = np_ // 2

    outer = pl.multiple_of((1 - c) * 0 + c * (LANES - OUT_W), 128)
    for k in range(1, K - 1):
        tb[k][:, pl.ds(outer, OUT_W)] = jnp.zeros((CH, OUT_W), BF)
    at_end = (line == 0) | (line == last)

    @pl.when(at_end)
    def _():
        tb0[:, pl.ds(outer, OUT_W)] = jnp.zeros((CH, OUT_W), BF)
        to = pl.multiple_of(c * OWN * 256, 128)
        ot[:, pl.ds(to, EXT * 256)] = jnp.zeros((8, EXT * 256), jnp.int32)
        wt[:, pl.ds(to, EXT * 256)] = jnp.zeros((8, EXT * 256), F32)

    msg[2 * OWN] = jnp.zeros((16, 128), BF)

    bar = pltpu.get_barrier_semaphore()
    for dn in (-1, 0, 1):
        for dc in (0, 1):
            for dg in (0, 1):
                pp = 2 * (n + dn) + dc

                @pl.when((n + dn >= 0) & (n + dn < ng) & ~((pp == p) & (dg == g)))
                def _():
                    pl.semaphore_signal(bar, inc=1, device_id=(pp, dg), device_id_type=MESH)

    def hello(i, carry):
        j = (i + p) % np_
        pp, gg = 2 * (j // 2) + g, j % 2

        @pl.when(~((pp == p) & (gg == g)))
        def _():
            pl.semaphore_signal(bar, inc=1, device_id=(pp, gg), device_id_type=MESH)
        return carry

    lax.fori_loop(0, np_, hello, 0)
    pl.semaphore_wait(bar, 11 - 4 * jnp.where((n == 0) | (n == ng - 1), 1, 0) + np_ - jnp.where(c == g, 1, 0))

    half = 4096
    main_dst = pl.multiple_of((1 - c) * EXT * 256, 128)
    ext_dst = pl.multiple_of(c * OWN * 256, 128)
    sib_dst = pl.multiple_of(c * EXT * 256, 128)

    def tables(fn):
        fn(0, offs, ot)
        fn(1, wts, wt)

    def tab_main_local(i, src, dst):
        return pltpu.make_async_copy(src.at[:, pl.ds(pl.multiple_of(c * half, 128), half)],
                                     dst.at[:, pl.ds(main_dst, half)], tab_l.at[i])

    def tab_main_remote(i, src, dst):
        return pltpu.make_async_remote_copy(
            src_ref=src.at[:, pl.ds(pl.multiple_of((1 - c) * half, 128), half)],
            dst_ref=dst.at[:, pl.ds(sib_dst, half)],
            send_sem=tab_s.at[i], recv_sem=tab_r.at[i], device_id=sib, device_id_type=MESH)

    def tab_ext_local(i, src, dst):
        return pltpu.make_async_copy(
            src.at[:, pl.ds(pl.multiple_of((1 - c) * (8192 - EXT * 256), 128), EXT * 256)],
            dst.at[:, pl.ds(ext_dst, EXT * 256)], tab_l.at[i])

    out_line = line - 1 + 2 * c
    outp, outg_ = place(out_line)
    has_out = ~at_end
    other_ext = pl.multiple_of((1 - c) * OWN * 256, 128)

    def tab_ext_remote(i, src, dst):
        return pltpu.make_async_remote_copy(
            src_ref=src.at[:, pl.ds(pl.multiple_of(c * (8192 - EXT * 256), 128), EXT * 256)],
            dst_ref=dst.at[:, pl.ds(other_ext, EXT * 256)],
            send_sem=tab_s.at[2 + i], recv_sem=tab_r.at[2 + i],
            device_id=(outp, outg_), device_id_type=MESH)

    @pl.when(home)
    def _():
        tables(lambda i, s, d: tab_main_local(i, s, d).start())
        tables(lambda i, s, d: tab_main_remote(i, s, d).start())

    @pl.when(~home)
    def _():
        tables(lambda i, s, d: tab_ext_local(i, s, d).start())

    row = pl.multiple_of(32 * g, 32)
    flows = (
        (2 * p, 0, HALO + 4096, LANES - HALO - 4096, 0),
        (2 * p + 1, 4096 - HALO, HALO + 4096, 0, 0),
        (2 * p - 1, 0, OUT_W, LANES - OUT_W, 2),
        (2 * p + 2, 8192 - OUT_W, OUT_W, 0, 2),
    )

    def flow_parts(i):
        target, src0, size, dst0, sem = flows[i]
        src = feat.at[:, pl.ds(src0, size)]
        dst = tb0.at[pl.ds(row, 32), pl.ds(dst0, size)]
        return target, src, dst, sem + g

    def flow_ok(i):
        target = flows[i][0]
        return (target >= 0) & (target <= last)

    def flow_remote(i):
        target, src, dst, sem = flow_parts(i)
        tp, tg = place(target)
        return pltpu.make_async_remote_copy(
            src_ref=src, dst_ref=dst, send_sem=t0_s.at[i], recv_sem=t0_r.at[sem],
            device_id=(tp, tg), device_id_type=MESH)

    for i in range(4):
        target, src, dst, sem = flow_parts(i)

        @pl.when(flow_ok(i) & (target == line))
        def _():
            pltpu.make_async_copy(src, dst, t0_r.at[sem]).start()

        @pl.when(flow_ok(i) & (target != line))
        def _():
            flow_remote(i).start()

    @pl.when(home & has_out)
    def _():
        tables(lambda i, s, d: tab_ext_remote(i, s, d).start())

    mixcat = jnp.concatenate([mix[k] for k in range(K)], axis=0)
    oi, oo = iota((64, 64), 0), iota((64, 64), 1)
    wanted = (oi // 16 % 2) * 32 + 2 * (oi % 16) + oi // 32
    perm = jnp.where(oo == wanted, 1.0, 0.0).astype(BF)
    mixall[g] = lax.dot_general(perm, mixcat, (((1,), (1,)), ((), ())),
                                preferred_element_type=F32).astype(BF)
    biasall[g] = jnp.zeros((8, 128), F32)
    biasall[g, 0:1, 0:32] = bias[...]

    rowv = jnp.broadcast_to(own_ref[...], (32, 32))
    si, sl = iota((32, 32), 0), iota((32, 32), 1)
    bi, bl = iota((32, 128), 0), iota((32, 128), 1)
    col = jnp.sum(jnp.where(si == sl, rowv, 0), axis=1, keepdims=True)
    same = (jnp.broadcast_to(col, (32, 32)) == rowv) & (sl < si)
    slot = jnp.sum(jnp.where(same, 1, 0), axis=1, keepdims=True)
    key = col * 2 + slot
    hit = jnp.sum(jnp.where(jnp.broadcast_to(key, (32, 128)) == bl, bi + 1, 0), axis=0, keepdims=True)
    inv[c] = jnp.broadcast_to(jnp.where(hit == 0, 2 * OWN, hit - 1), (8, 128))

    par = [
        pltpu.make_async_remote_copy(src_ref=mixall.at[g], dst_ref=mixall.at[g], send_sem=par_s.at[0],
                                     recv_sem=par_r.at[0], device_id=partner, device_id_type=MESH),
        pltpu.make_async_remote_copy(src_ref=biasall.at[g], dst_ref=biasall.at[g], send_sem=par_s.at[1],
                                     recv_sem=par_r.at[1], device_id=partner, device_id_type=MESH),
        pltpu.make_async_remote_copy(src_ref=inv.at[c], dst_ref=inv.at[c], send_sem=par_s.at[2],
                                     recv_sem=par_r.at[2], device_id=sib, device_id_type=MESH),
    ]
    for cp in par:
        cp.start()

    def block_of(i):
        return c * i + (1 - c) * (NB - 1 - i)

    base = [(iota((16, 256), 0) + 16 * r).astype(jnp.int16) for r in range(16)]

    def build(i, carry):
        b = block_of(i)
        lanes = pl.ds(pl.multiple_of(256 * b, 256), 256)
        s = iota((8, 256), 1) + ot[:, lanes] + 512
        w = wt[:, lanes]
        cl = jnp.sum(jnp.where(s == -1, w, 0.0), axis=0, keepdims=True)
        cr = jnp.sum(jnp.where(s == WIN, w, 0.0), axis=0, keepdims=True)
        cor[b, 0:1, :] = cl
        cor[b, 1:2, :] = cr
        full = w
        for r in range(1, 8):
            full = full + jnp.where(s == pltpu.roll(s, r, 0), pltpu.roll(w, r, 0), 0.0)
        for j in range(8):
            s16[j] = jnp.broadcast_to(s[j:j + 1], (16, 256)).astype(jnp.int16)
            w16[j] = jnp.broadcast_to(full[j:j + 1], (16, 256)).astype(BF)
        for q in range(WIN // 256):
            acc = [jnp.zeros((16, 256), BF)] * 16
            for j in range(8):
                sq = s16[j] - jnp.int16(256 * q)
                wq = w16[j]
                acc = [jnp.where(base[r] == sq, wq, acc[r]) for r in range(16)]
            for r in range(16):
                wm[b, 256 * q + 16 * r:256 * q + 16 * (r + 1), :] = acc[r]
        return carry

    lo1 = jnp.where(home, 0, OWN)
    hi1 = jnp.where(home, OWN, NB)
    lo2 = jnp.where(home, OWN, 0)
    hi2 = jnp.where(home, NB, OWN)

    @pl.when(home)
    def _():
        tables(lambda i, s, d: tab_main_local(i, s, d).wait())

    @pl.when(~home)
    def _():
        tables(lambda i, s, d: tab_ext_local(i, s, d).wait())

    lax.fori_loop(lo1, hi1, build, 0)

    @pl.when(~home)
    def _():
        tables(lambda i, s, d: pltpu.make_async_copy(
            s.at[:, pl.ds(0, half)], d.at[:, pl.ds(main_dst, half)], tab_r.at[i]).wait())

    @pl.when(home & has_out)
    def _():
        tables(lambda i, s, d: pltpu.make_async_copy(
            s.at[:, pl.ds(0, EXT * 256)], d.at[:, pl.ds(ext_dst, EXT * 256)], tab_r.at[2 + i]).wait())

    lax.fori_loop(lo2, hi2, build, 0)

    main_at = pl.multiple_of((1 - c) * (LANES - HALO - 4096), 128)
    for gg in range(2):
        pltpu.make_async_copy(feat.at[:, pl.ds(0, HALO + 4096)],
                              tb0.at[pl.ds(32 * gg, 32), pl.ds(main_at, HALO + 4096)],
                              t0_r.at[gg]).wait()

    def term(k, i):
        b = block_of(i)
        at = pl.multiple_of(256 * b, 256)
        src = tb[k - 1]
        u = jnp.dot(src[:, pl.ds(at + 128, WIN)], wm[b], preferred_element_type=F32)
        left = pltpu.roll(src[:, pl.ds(at, 128)].astype(F32), 1, 1)
        right = pltpu.roll(src[:, pl.ds(at + 1408, 128)].astype(F32), 127, 1)
        u = u + jnp.concatenate([left * cor[b, 0:1, 0:128], right * cor[b, 1:2, 128:256]], axis=1)
        if k == 1:
            t = u
        elif k == 2:
            t = 2.0 * u - tb0[:, pl.ds(at + HALO, 256)].astype(F32)
        else:
            t = 2.0 * u - fp[k % 2][:, pl.ds(at, 256)]
        return at, t

    def run(k, lo, hi, group=10):
        def one(i):
            at, t = term(k, i)
            fp[k % 2][:, pl.ds(at, 256)] = t
            tb[k][:, pl.ds(at + HALO, 256)] = t.astype(BF)

        full = (hi - lo) // group

        def some(m, carry):
            for r in range(group):
                one(lo + m * group + r)
            return carry

        first = lo
        if full > 1:
            lax.fori_loop(0, full, some, 0)
            first = lo + full * group
        for i in range(first, hi):
            one(i)

    own_at = HALO + (1 - c) * EXT * 256
    edge_src = pl.multiple_of(own_at + (1 - c) * (4096 - HALO), 128)
    edge_dst = pl.multiple_of(c * (LANES - HALO), 128)

    def inner(k):
        return pltpu.make_async_remote_copy(
            src_ref=tb[k].at[:, pl.ds(edge_src, HALO)], dst_ref=tb[k].at[:, pl.ds(edge_dst, HALO)],
            send_sem=in_s.at[k], recv_sem=in_r.at[k], device_id=sib, device_id_type=MESH)

    def outer_copy(k, width, m):
        src = pl.multiple_of(own_at + c * (4096 - width), 128)
        if k == 3:
            dst = x3.at[:, :]
        else:
            dst = tb[k].at[:, pl.ds(pl.multiple_of((1 - c) * (LANES - OUT_W) + c * (OUT_W - width), 128), width)]
        return pltpu.make_async_remote_copy(
            src_ref=tb[k].at[:, pl.ds(src, width)], dst_ref=dst,
            send_sem=mid_s.at[m], recv_sem=mid_r.at[m], device_id=(outp, outg_), device_id_type=MESH)

    run(1, 0, 3)
    inner(1).start()
    run(1, 3, 13)

    @pl.when(has_out)
    def _():
        for gg in range(2):
            pltpu.make_async_copy(feat.at[:, pl.ds(0, OUT_W)],
                                  tb0.at[pl.ds(32 * gg, 32), pl.ds(outer, OUT_W)],
                                  t0_r.at[2 + gg]).wait()

    run(1, 13, 23)
    inner(1).wait_recv()
    run(2, 0, 3)
    inner(2).start()
    run(2, 3, 21)
    inner(2).wait_recv()
    run(3, 0, 3)
    inner(3).start()
    run(3, 3, 19)

    @pl.when(has_out)
    def _():
        outer_copy(3, S3, 0).start()

    run(4, 9, 16)

    @pl.when(has_out)
    def _():
        outer_copy(4, S4, 1).start()

    pltpu.make_async_copy(mixall.at[1 - g], mixall.at[1 - g], par_r.at[0]).wait()
    pltpu.make_async_copy(biasall.at[1 - g], biasall.at[1 - g], par_r.at[1]).wait()
    pltpu.make_async_copy(inv.at[1 - c], inv.at[1 - c], par_r.at[2]).wait()
    to_smem = pltpu.make_async_copy(inv.at[gx], inv_s, loc.at[0])
    to_smem.start()
    o1, l1 = iota((64, 128), 0), iota((64, 128), 1)
    brow = jnp.where(o1 // 16 % 2 == 0, biasall[0, 0:1, :], biasall[1, 0:1, :])
    bcol = jnp.sum(jnp.where(l1 == 2 * (o1 % 16) + o1 // 32, brow, 0.0), axis=1, keepdims=True)
    pi, pq = iota((512, 128), 0), iota((512, 128), 1)
    pool = jnp.where(pi % 256 // 4 + 64 * (pi // 256) == pq, 0.25, 0.0).astype(BF)
    to_smem.wait()

    inner(3).wait_recv()
    run(4, 0, 3)
    inner(4).start()
    run(4, 3, 9)
    inner(4).wait_recv()
    run(5, 0, 3)
    inner(5).start()
    run(5, 3, 13)
    inner(5).wait_recv()
    run(6, 0, 3)
    inner(6).start()
    run(6, 3, 10)
    inner(6).wait_recv()

    def finish(i):
        at, t = term(7, i)
        t = t.astype(BF)
        total = bcol
        for gg in range(2):
            rows = slice(32 * gg, 32 * gg + 32)
            rhs = jnp.concatenate([tb[k][rows, pl.ds(at + HALO, 256)] for k in range(K - 1)] + [t[rows]], axis=0)
            part = jnp.dot(mixall[gg], rhs, preferred_element_type=F32)
            total = total + part.astype(BF).astype(F32)
        filt = jnp.maximum(total, 0.0).astype(BF)
        lhs = jnp.concatenate([filt[0:32], filt[32:64]], axis=1)
        pooled = jnp.dot(lhs, pool, preferred_element_type=F32)
        b = block_of(i) - (1 - c) * EXT
        msg[c * OWN + b] = jnp.where(c == 0, pooled[0:16], pooled[16:32]).astype(BF)
        snd[b] = jnp.where(c == 0, pooled[16:32], pooled[0:16]).astype(BF)

    def swap(m):
        b0 = c * 8 * m + (1 - c) * (8 - 8 * m)
        return pltpu.make_async_remote_copy(
            src_ref=snd.at[pl.ds(b0, 8)], dst_ref=msg.at[pl.ds(c * OWN + b0, 8)],
            send_sem=sw_s.at[m], recv_sem=sw_r.at[m], device_id=sib, device_id_type=MESH)

    for i in range(0, 7):
        finish(i)

    @pl.when(has_out)
    def _():
        outer_copy(3, S3, 0).wait_recv()
        outer_copy(4, S4, 1).wait_recv()
        d3 = pl.multiple_of((1 - c) * (EXT * 256 - S3) + c * OWN * 256, 128)
        fp1[:, pl.ds(d3, S3)] = x3[...].astype(F32)
        d4 = pl.multiple_of((1 - c) * (EXT * 256 - 768) + c * OWN * 256, 128)
        fp0[:, pl.ds(d4, 768)] = tb4[:, pl.ds(d4 + HALO, 768)].astype(F32)

    run(5, 13, 21)
    run(6, 10, 19)
    finish(7)
    swap(0).start()
    for i in range(8, 16):
        finish(i)
    swap(1).start()
    for m in range(2):
        pltpu.make_async_copy(msg.at[pl.ds((1 - c) * OWN + 8 * m, 8)],
                              msg.at[pl.ds((1 - c) * OWN + 8 * m, 8)], sw_r.at[m]).wait()

    ei, ej = iota((32, 32), 0), iota((32, 32), 1)
    weave = jnp.where(ej == (ei % 2) * 16 + ei // 2, 1.0, 0.0).astype(BF)
    src_patch = 2 * n + gx

    def assemble(i, carry):
        m = (i + p // 4) % (np_ // 4)
        cols = []
        for r in range(4):
            o = 4 * m + r
            cols.append(jnp.concatenate([msg[inv_s[0, 2 * o]], msg[inv_s[0, 2 * o + 1]]], axis=0))
        res = jnp.dot(weave, jnp.concatenate(cols, axis=1), preferred_element_type=F32).astype(BF)
        for r in range(4):
            outg[4 * m + r] = res[:, 128 * r:128 * (r + 1)]
        for r in range(4):
            o = 4 * m + r
            me = (o == p) & (c == g)

            @pl.when(me)
            def _():
                pltpu.make_async_copy(outg.at[o], out_ref.at[src_patch], all_r.at[0]).start()

            @pl.when(~me)
            def _():
                pltpu.make_async_remote_copy(
                    src_ref=outg.at[o], dst_ref=out_ref.at[src_patch], send_sem=all_s.at[0],
                    recv_sem=all_r.at[0], device_id=(o, c), device_id_type=MESH).start()
        return carry

    lax.fori_loop(0, np_ // 4, assemble, 0)

    @pl.when(home)
    def _():
        tables(lambda i, s, d: tab_main_remote(i, s, d).wait_send())

    @pl.when(home & has_out)
    def _():
        tables(lambda i, s, d: tab_ext_remote(i, s, d).wait_send())

    for i in range(4):
        @pl.when(flow_ok(i) & (flows[i][0] != line))
        def _():
            flow_remote(i).wait_send()

    for cp in par:
        cp.wait_send()
    for k in range(1, K - 1):
        inner(k).wait_send()

    @pl.when(has_out)
    def _():
        outer_copy(3, S3, 0).wait_send()
        outer_copy(4, S4, 1).wait_send()

    for m in range(2):
        swap(m).wait_send()

    pltpu.make_async_copy(out_ref.at[:], out_ref.at[:], all_r.at[0]).wait()
    pltpu.make_async_copy(outg.at[pl.ds(0, np_ - 1)], outg.at[pl.ds(0, np_ - 1)], all_s.at[0]).wait()

    @pl.when(c != g)
    def _():
        pltpu.make_async_copy(outg.at[0], outg.at[0], all_s.at[0]).wait()


def body(features, offsets, edge_weights, mix, bias, owners):
    np_ = lax.axis_size("patch")
    any_, vmem = pl.BlockSpec(memory_space=pl.ANY), pl.BlockSpec(memory_space=pltpu.VMEM)
    dma, vm = pltpu.SemaphoreType.DMA, pltpu.VMEM
    got = pl.pallas_call(
        functools.partial(cheb_kernel, np_),
        out_shape=jax.ShapeDtypeStruct((np_, 32, 128), BF),
        in_specs=[any_, any_, any_, vmem, vmem, vmem],
        out_specs=vmem,
        scratch_shapes=[
            *[vm((CH, LANES), BF)] * (K - 1), *[vm((CH, NPX), F32)] * 2, vm((NB, WIN, 256), BF),
            vm((8, NPX), jnp.int32), vm((8, NPX), F32), vm((NB, 8, 256), F32),
            vm((8, 16, 256), jnp.int16), vm((8, 16, 256), BF), vm((CH, S3), BF),
            vm((2, 64, 256), BF), vm((2, 8, 128), F32), vm((2, 8, 128), jnp.int32),
            pltpu.SMEM((8, 128), jnp.int32),
            vm((2 * OWN + 1, 16, 128), BF), vm((OWN, 16, 128), BF), vm((np_, 32, 128), BF),
            dma((4,)), dma((4,)), dma((2,)), dma((4,)), dma((4,)), dma((3,)), dma((3,)),
            dma((K,)), dma((K,)), dma((2,)), dma((2,)), dma((2,)), dma((2,)), dma((1,)),
            dma((1,)), dma((1,)),
        ],
        compiler_params=pltpu.CompilerParams(
            vmem_limit_bytes=62 << 20, collective_id=0, has_side_effects=True),
        name="cheb",
    )(features, offsets, edge_weights, mix.transpose(0, 2, 1), bias.reshape(1, -1), owners.reshape(1, -1))
    got = got.reshape(np_, 16, 2, 128).transpose(0, 2, 1, 3).reshape(np_, 2, 2048)
    return got[None]


def solution(mesh):
    return jax.shard_map(
        body,
        mesh=mesh,
        in_specs=(
            P("chan", "patch"),
            P(None, "patch"),
            P(None, "patch"),
            P(None, None, "chan"),
            P("chan"),
            P("patch", None),
        ),
        out_specs=P("patch", None, None, "chan"),
        check_vma=False,
    )
```

```python
import functools

import jax
import jax.numpy as jnp
from jax import lax
from jax.experimental import pallas as pl
from jax.experimental.pallas import tpu as pltpu
from jax.sharding import PartitionSpec as P

MESH = pl.DeviceIdType.MESH
BF = jnp.bfloat16
F32 = jnp.float32
K = 8
CH = 64
OWN = 16
EXT = 5
NB = OWN + EXT
HALO = 640
LANES = HALO + NB * 256 + HALO
OUT_W = EXT * 256 + HALO
WIN = 1280
NPX = NB * 256
MID = 1152


def place(line):
    n, q = line // 4, line % 4
    return 2 * n + q % 2, (q // 2 + n % 2) % 2


def iota(shape, dim):
    return lax.broadcasted_iota(jnp.int32, shape, dim)


def cheb_kernel(np_, feat, offs, wts, mix, bias, own_ref, out_ref,
                tb0, tb1, tb2, tb3, tb4, tb5, tb6, fp0, fp1,
                wm, ot, wt, cor, s16, w16, mixall, biasall, inv, inv_s,
                msg, snd, outg, plhs, t0_s, t0_r, tab_l, tab_s, tab_r, par_s, par_r,
                in_s, in_r, mid_s, mid_r, sw_s, sw_r, loc, all_s, all_r):
    tb = (tb0, tb1, tb2, tb3, tb4, tb5, tb6)
    fp = (fp0, fp1)
    p = lax.axis_index("patch")
    g = lax.axis_index("chan")
    n, c = p // 2, p % 2
    gx = (g + n) % 2
    line = 4 * n + 2 * gx + c
    last = 2 * np_ - 1
    sib = (p + 1 - 2 * c, g)
    partner = (p, 1 - g)
    first_core = c == 0
    home = gx == c
    ng = np_ // 2

    outer = pl.multiple_of((1 - c) * 0 + c * (LANES - OUT_W), 128)
    for k in range(1, K - 1):
        tb[k][:, pl.ds(outer, OUT_W)] = jnp.zeros((CH, OUT_W), BF)
    at_end = (line == 0) | (line == last)

    @pl.when(at_end)
    def _():
        tb0[:, pl.ds(outer, OUT_W)] = jnp.zeros((CH, OUT_W), BF)
        to = pl.multiple_of(c * OWN * 256, 128)
        ot[:, pl.ds(to, EXT * 256)] = jnp.zeros((8, EXT * 256), jnp.int32)
        wt[:, pl.ds(to, EXT * 256)] = jnp.zeros((8, EXT * 256), F32)

    msg[2 * OWN] = jnp.zeros((16, 128), BF)

    bar = pltpu.get_barrier_semaphore()
    for dn in (-1, 0, 1):
        for dc in (0, 1):
            for dg in (0, 1):
                pp = 2 * (n + dn) + dc

                @pl.when((n + dn >= 0) & (n + dn < ng) & ~((pp == p) & (dg == g)))
                def _():
                    pl.semaphore_signal(bar, inc=1, device_id=(pp, dg), device_id_type=MESH)

    def hello(i, carry):
        j = (i + p) % np_
        pp, gg = 2 * (j // 2) + g, j % 2

        @pl.when(~((pp == p) & (gg == g)))
        def _():
            pl.semaphore_signal(bar, inc=1, device_id=(pp, gg), device_id_type=MESH)
        return carry

    lax.fori_loop(0, np_, hello, 0)
    pl.semaphore_wait(bar, 11 - 4 * jnp.where((n == 0) | (n == ng - 1), 1, 0) + np_ - jnp.where(c == g, 1, 0))

    half = 4096
    main_dst = pl.multiple_of((1 - c) * EXT * 256, 128)
    ext_dst = pl.multiple_of(c * OWN * 256, 128)
    sib_dst = pl.multiple_of(c * EXT * 256, 128)

    def tables(fn):
        fn(0, offs, ot)
        fn(1, wts, wt)

    def tab_main_local(i, src, dst):
        return pltpu.make_async_copy(src.at[:, pl.ds(pl.multiple_of(c * half, 128), half)],
                                     dst.at[:, pl.ds(main_dst, half)], tab_l.at[i])

    def tab_main_remote(i, src, dst):
        return pltpu.make_async_remote_copy(
            src_ref=src.at[:, pl.ds(pl.multiple_of((1 - c) * half, 128), half)],
            dst_ref=dst.at[:, pl.ds(sib_dst, half)],
            send_sem=tab_s.at[i], recv_sem=tab_r.at[i], device_id=sib, device_id_type=MESH)

    def tab_ext_local(i, src, dst):
        return pltpu.make_async_copy(
            src.at[:, pl.ds(pl.multiple_of((1 - c) * (8192 - EXT * 256), 128), EXT * 256)],
            dst.at[:, pl.ds(ext_dst, EXT * 256)], tab_l.at[i])

    out_line = line - 1 + 2 * c
    outp, outg_ = place(out_line)
    has_out = ~at_end
    other_ext = pl.multiple_of((1 - c) * OWN * 256, 128)

    def tab_ext_remote(i, src, dst):
        return pltpu.make_async_remote_copy(
            src_ref=src.at[:, pl.ds(pl.multiple_of(c * (8192 - EXT * 256), 128), EXT * 256)],
            dst_ref=dst.at[:, pl.ds(other_ext, EXT * 256)],
            send_sem=tab_s.at[2 + i], recv_sem=tab_r.at[2 + i],
            device_id=(outp, outg_), device_id_type=MESH)

    @pl.when(home)
    def _():
        tables(lambda i, s, d: tab_main_local(i, s, d).start())
        tables(lambda i, s, d: tab_main_remote(i, s, d).start())

    @pl.when(~home)
    def _():
        tables(lambda i, s, d: tab_ext_local(i, s, d).start())

    row = pl.multiple_of(32 * g, 32)
    flows = (
        (2 * p, 0, HALO + 4096, LANES - HALO - 4096, 0),
        (2 * p + 1, 4096 - HALO, HALO + 4096, 0, 0),
        (2 * p - 1, 0, OUT_W, LANES - OUT_W, 2),
        (2 * p + 2, 8192 - OUT_W, OUT_W, 0, 2),
    )

    def flow_parts(i):
        target, src0, size, dst0, sem = flows[i]
        src = feat.at[:, pl.ds(src0, size)]
        dst = tb0.at[pl.ds(row, 32), pl.ds(dst0, size)]
        return target, src, dst, sem + g

    def flow_ok(i):
        target = flows[i][0]
        return (target >= 0) & (target <= last)

    def flow_remote(i):
        target, src, dst, sem = flow_parts(i)
        tp, tg = place(target)
        return pltpu.make_async_remote_copy(
            src_ref=src, dst_ref=dst, send_sem=t0_s.at[i], recv_sem=t0_r.at[sem],
            device_id=(tp, tg), device_id_type=MESH)

    for i in range(4):
        target, src, dst, sem = flow_parts(i)

        @pl.when(flow_ok(i) & (target == line))
        def _():
            pltpu.make_async_copy(src, dst, t0_r.at[sem]).start()

        @pl.when(flow_ok(i) & (target != line))
        def _():
            flow_remote(i).start()

    @pl.when(home & has_out)
    def _():
        tables(lambda i, s, d: tab_ext_remote(i, s, d).start())

    mixcat = jnp.concatenate([mix[k] for k in range(K)], axis=0)
    oi, oo = iota((64, 64), 0), iota((64, 64), 1)
    wanted = (oi // 16 % 2) * 32 + 2 * (oi % 16) + oi // 32
    perm = jnp.where(oo == wanted, 1.0, 0.0).astype(BF)
    mixall[g] = lax.dot_general(perm, mixcat, (((1,), (1,)), ((), ())),
                                preferred_element_type=F32).astype(BF)
    biasall[g] = jnp.zeros((8, 128), F32)
    biasall[g, 0:1, 0:32] = bias[...]

    rowv = jnp.broadcast_to(own_ref[...], (32, 32))
    si, sl = iota((32, 32), 0), iota((32, 32), 1)
    bi, bl = iota((32, 128), 0), iota((32, 128), 1)
    col = jnp.sum(jnp.where(si == sl, rowv, 0), axis=1, keepdims=True)
    same = (jnp.broadcast_to(col, (32, 32)) == rowv) & (sl < si)
    slot = jnp.sum(jnp.where(same, 1, 0), axis=1, keepdims=True)
    key = col * 2 + slot
    hit = jnp.sum(jnp.where(jnp.broadcast_to(key, (32, 128)) == bl, bi + 1, 0), axis=0, keepdims=True)
    inv[c] = jnp.broadcast_to(jnp.where(hit == 0, 2 * OWN, hit - 1), (8, 128))

    par = [
        pltpu.make_async_remote_copy(src_ref=mixall.at[g], dst_ref=mixall.at[g], send_sem=par_s.at[0],
                                     recv_sem=par_r.at[0], device_id=partner, device_id_type=MESH),
        pltpu.make_async_remote_copy(src_ref=biasall.at[g], dst_ref=biasall.at[g], send_sem=par_s.at[1],
                                     recv_sem=par_r.at[1], device_id=partner, device_id_type=MESH),
        pltpu.make_async_remote_copy(src_ref=inv.at[c], dst_ref=inv.at[c], send_sem=par_s.at[2],
                                     recv_sem=par_r.at[2], device_id=sib, device_id_type=MESH),
    ]
    for cp in par:
        cp.start()

    def block_of(i):
        return c * i + (1 - c) * (NB - 1 - i)

    base = [(iota((16, 256), 0) + 16 * r).astype(jnp.int16) for r in range(16)]

    def build(i, carry):
        b = block_of(i)
        lanes = pl.ds(pl.multiple_of(256 * b, 256), 256)
        s = iota((8, 256), 1) + ot[:, lanes] + 512
        w = wt[:, lanes]
        cl = jnp.sum(jnp.where(s == -1, w, 0.0), axis=0, keepdims=True)
        cr = jnp.sum(jnp.where(s == WIN, w, 0.0), axis=0, keepdims=True)
        cor[b, 0:1, :] = cl
        cor[b, 1:2, :] = cr
        full = w
        for r in range(1, 8):
            full = full + jnp.where(s == pltpu.roll(s, r, 0), pltpu.roll(w, r, 0), 0.0)
        for j in range(8):
            s16[j] = jnp.broadcast_to(s[j:j + 1], (16, 256)).astype(jnp.int16)
            w16[j] = jnp.broadcast_to(full[j:j + 1], (16, 256)).astype(BF)
        for q in range(WIN // 256):
            acc = [jnp.zeros((16, 256), BF)] * 16
            for j in range(8):
                sq = s16[j] - jnp.int16(256 * q)
                wq = w16[j]
                acc = [jnp.where(base[r] == sq, wq, acc[r]) for r in range(16)]
            for r in range(16):
                wm[b, 256 * q + 16 * r:256 * q + 16 * (r + 1), :] = acc[r]
        return carry

    lo1 = jnp.where(home, 0, OWN)
    hi1 = jnp.where(home, OWN, NB)
    lo2 = jnp.where(home, OWN, 0)
    hi2 = jnp.where(home, NB, OWN)

    @pl.when(home)
    def _():
        tables(lambda i, s, d: tab_main_local(i, s, d).wait())

    @pl.when(~home)
    def _():
        tables(lambda i, s, d: tab_ext_local(i, s, d).wait())

    lax.fori_loop(lo1, hi1, build, 0)

    @pl.when(~home)
    def _():
        tables(lambda i, s, d: pltpu.make_async_copy(
            s.at[:, pl.ds(0, half)], d.at[:, pl.ds(main_dst, half)], tab_r.at[i]).wait())

    @pl.when(home & has_out)
    def _():
        tables(lambda i, s, d: pltpu.make_async_copy(
            s.at[:, pl.ds(0, EXT * 256)], d.at[:, pl.ds(ext_dst, EXT * 256)], tab_r.at[2 + i]).wait())

    lax.fori_loop(lo2, hi2, build, 0)

    main_at = pl.multiple_of((1 - c) * (LANES - HALO - 4096), 128)
    for gg in range(2):
        pltpu.make_async_copy(feat.at[:, pl.ds(0, HALO + 4096)],
                              tb0.at[pl.ds(32 * gg, 32), pl.ds(main_at, HALO + 4096)],
                              t0_r.at[gg]).wait()

    def term(k, i):
        b = block_of(i)
        at = pl.multiple_of(256 * b, 256)
        src = tb[k - 1]
        win = src[:, pl.ds(at + 128, WIN)]
        left = pltpu.roll(src[:, pl.ds(at, 128)].astype(F32), 1, 1)
        right = pltpu.roll(src[:, pl.ds(at + 1408, 128)].astype(F32), 127, 1)
        u0 = jnp.dot(win, wm[b, :, 0:128], preferred_element_type=F32) + left * cor[b, 0:1, 0:128]
        u1 = jnp.dot(win, wm[b, :, 128:256], preferred_element_type=F32) + right * cor[b, 1:2, 128:256]
        u = jnp.concatenate([u0, u1], axis=1)
        if k == 1:
            t = u
        elif k == 2:
            t = 2.0 * u - tb0[:, pl.ds(at + HALO, 256)].astype(F32)
        else:
            t = 2.0 * u - fp[k % 2][:, pl.ds(at, 256)]
        return at, t

    def run(k, lo, hi, group=10):
        def one(i):
            at, t = term(k, i)
            fp[k % 2][:, pl.ds(at, 256)] = t
            tb[k][:, pl.ds(at + HALO, 256)] = t.astype(BF)

        full = (hi - lo) // group

        def some(m, carry):
            for r in range(group):
                one(lo + m * group + r)
            return carry

        first = lo
        if full > 1:
            lax.fori_loop(0, full, some, 0)
            first = lo + full * group
        for i in range(first, hi):
            one(i)

    own_at = HALO + (1 - c) * EXT * 256
    edge_src = pl.multiple_of(own_at + (1 - c) * (4096 - HALO), 128)
    edge_dst = pl.multiple_of(c * (LANES - HALO), 128)

    def inner(k):
        return pltpu.make_async_remote_copy(
            src_ref=tb[k].at[:, pl.ds(edge_src, HALO)], dst_ref=tb[k].at[:, pl.ds(edge_dst, HALO)],
            send_sem=in_s.at[k], recv_sem=in_r.at[k], device_id=sib, device_id_type=MESH)

    def mid(k):
        src = pl.multiple_of(own_at + c * (4096 - MID), 128)
        dst = pl.multiple_of((1 - c) * (LANES - OUT_W) + c * (OUT_W - MID), 128)
        return pltpu.make_async_remote_copy(
            src_ref=tb[k].at[:, pl.ds(src, MID)], dst_ref=tb[k].at[:, pl.ds(dst, MID)],
            send_sem=mid_s.at[k // 4], recv_sem=mid_r.at[k // 4], device_id=(outp, outg_), device_id_type=MESH)

    run(1, 0, 3)
    inner(1).start()
    run(1, 3, 13)

    @pl.when(has_out)
    def _():
        for gg in range(2):
            pltpu.make_async_copy(feat.at[:, pl.ds(0, OUT_W)],
                                  tb0.at[pl.ds(32 * gg, 32), pl.ds(outer, OUT_W)],
                                  t0_r.at[2 + gg]).wait()

    run(1, 13, NB)
    inner(1).wait_recv()
    run(2, 0, 3)
    inner(2).start()
    run(2, 3, 19)
    inner(2).wait_recv()
    run(3, 11, 16)

    @pl.when(has_out)
    def _():
        mid(3).start()

    pltpu.make_async_copy(mixall.at[1 - g], mixall.at[1 - g], par_r.at[0]).wait()
    pltpu.make_async_copy(biasall.at[1 - g], biasall.at[1 - g], par_r.at[1]).wait()
    pltpu.make_async_copy(inv.at[1 - c], inv.at[1 - c], par_r.at[2]).wait()
    to_smem = pltpu.make_async_copy(inv.at[gx], inv_s, loc.at[0])
    to_smem.start()
    o1, l1 = iota((64, 128), 0), iota((64, 128), 1)
    brow = jnp.where(o1 // 16 % 2 == 0, biasall[0, 0:1, :], biasall[1, 0:1, :])
    bcol = jnp.sum(jnp.where(l1 == 2 * (o1 % 16) + o1 // 32, brow, 0.0), axis=1, keepdims=True)
    pi, pq = iota((512, 128), 0), iota((512, 128), 1)
    pool = jnp.where(pi % 256 // 4 + 64 * (pi // 256) == pq, 0.25, 0.0).astype(BF)
    to_smem.wait()

    run(3, 0, 3)
    inner(3).start()
    run(3, 3, 11)
    inner(3).wait_recv()
    run(4, 0, 3)
    inner(4).start()
    run(4, 3, 13)
    inner(4).wait_recv()
    run(5, 0, 3)
    inner(5).start()
    run(5, 3, 10)
    inner(5).wait_recv()
    run(6, 0, 3)
    inner(6).start()

    @pl.when(has_out)
    def _():
        mid(3).wait_recv()

    run(4, 13, 19)
    run(5, 10, 16)

    @pl.when(has_out)
    def _():
        mid(5).start()

    run(6, 3, 13)
    inner(6).wait_recv()

    def finish(i):
        at, t = term(7, i)
        t = t.astype(BF)
        total = bcol
        for gg in range(2):
            rows = slice(32 * gg, 32 * gg + 32)
            rhs = jnp.concatenate([tb[k][rows, pl.ds(at + HALO, 256)] for k in range(K - 1)] + [t[rows]], axis=0)
            part = jnp.dot(mixall[gg], rhs, preferred_element_type=F32)
            total = total + part.astype(BF).astype(F32)
        filt = jnp.maximum(total, 0.0).astype(BF)
        plhs[32 * i:32 * i + 32, 0:256] = filt[0:32]
        plhs[32 * i:32 * i + 32, 256:512] = filt[32:64]

    def pool_blocks(m):
        pooled = jnp.dot(plhs[256 * m:256 * m + 256, :], pool, preferred_element_type=F32)
        for r in range(8):
            b = block_of(8 * m + r) - (1 - c) * EXT
            even, odd = pooled[32 * r:32 * r + 16], pooled[32 * r + 16:32 * r + 32]
            msg[c * OWN + b] = jnp.where(c == 0, even, odd).astype(BF)
            snd[b] = jnp.where(c == 0, odd, even).astype(BF)

    def swap(m):
        b0 = c * 8 * m + (1 - c) * (8 - 8 * m)
        return pltpu.make_async_remote_copy(
            src_ref=snd.at[pl.ds(b0, 8)], dst_ref=msg.at[pl.ds(c * OWN + b0, 8)],
            send_sem=sw_s.at[m], recv_sem=sw_r.at[m], device_id=sib, device_id_type=MESH)

    for i in range(0, 8):
        finish(i)
    pool_blocks(0)
    swap(0).start()
    for i in range(8, 10):
        finish(i)

    @pl.when(has_out)
    def _():
        mid(5).wait_recv()

    run(6, 13, 19)
    for i in range(10, 16):
        finish(i)
    pool_blocks(1)
    swap(1).start()
    for m in range(2):
        pltpu.make_async_copy(msg.at[pl.ds((1 - c) * OWN + 8 * m, 8)],
                              msg.at[pl.ds((1 - c) * OWN + 8 * m, 8)], sw_r.at[m]).wait()

    ei, ej = iota((32, 32), 0), iota((32, 32), 1)
    weave = jnp.where(ej == (ei % 2) * 16 + ei // 2, 1.0, 0.0).astype(BF)
    src_patch = 2 * n + gx

    def assemble(i, carry):
        m = (i + p // 4) % (np_ // 4)
        cols = []
        for r in range(4):
            o = 4 * m + r
            cols.append(jnp.concatenate([msg[inv_s[0, 2 * o]], msg[inv_s[0, 2 * o + 1]]], axis=0))
        res = jnp.dot(weave, jnp.concatenate(cols, axis=1), preferred_element_type=F32).astype(BF)
        for r in range(4):
            outg[4 * m + r] = res[:, 128 * r:128 * (r + 1)]
        for r in range(4):
            o = 4 * m + r
            me = (o == p) & (c == g)

            @pl.when(me)
            def _():
                pltpu.make_async_copy(outg.at[o], out_ref.at[src_patch], all_r.at[0]).start()

            @pl.when(~me)
            def _():
                pltpu.make_async_remote_copy(
                    src_ref=outg.at[o], dst_ref=out_ref.at[src_patch], send_sem=all_s.at[0],
                    recv_sem=all_r.at[0], device_id=(o, c), device_id_type=MESH).start()
        return carry

    lax.fori_loop(0, np_ // 4, assemble, 0)

    @pl.when(home)
    def _():
        tables(lambda i, s, d: tab_main_remote(i, s, d).wait_send())

    @pl.when(home & has_out)
    def _():
        tables(lambda i, s, d: tab_ext_remote(i, s, d).wait_send())

    for i in range(4):
        @pl.when(flow_ok(i) & (flows[i][0] != line))
        def _():
            flow_remote(i).wait_send()

    for cp in par:
        cp.wait_send()
    for k in range(1, K - 1):
        inner(k).wait_send()

    @pl.when(has_out)
    def _():
        mid(3).wait_send()
        mid(5).wait_send()

    for m in range(2):
        swap(m).wait_send()

    pltpu.make_async_copy(out_ref.at[:], out_ref.at[:], all_r.at[0]).wait()
    pltpu.make_async_copy(outg.at[pl.ds(0, np_ - 1)], outg.at[pl.ds(0, np_ - 1)], all_s.at[0]).wait()

    @pl.when(c != g)
    def _():
        pltpu.make_async_copy(outg.at[0], outg.at[0], all_s.at[0]).wait()


def body(features, offsets, edge_weights, mix, bias, owners):
    np_ = lax.axis_size("patch")
    any_, vmem = pl.BlockSpec(memory_space=pl.ANY), pl.BlockSpec(memory_space=pltpu.VMEM)
    dma, vm = pltpu.SemaphoreType.DMA, pltpu.VMEM
    got = pl.pallas_call(
        functools.partial(cheb_kernel, np_),
        out_shape=jax.ShapeDtypeStruct((np_, 32, 128), BF),
        in_specs=[any_, any_, any_, vmem, vmem, vmem],
        out_specs=vmem,
        scratch_shapes=[
            *[vm((CH, LANES), BF)] * (K - 1), *[vm((CH, NPX), F32)] * 2, vm((NB, WIN, 256), BF),
            vm((8, NPX), jnp.int32), vm((8, NPX), F32), vm((NB, 8, 256), F32),
            vm((8, 16, 256), jnp.int16), vm((8, 16, 256), BF),
            vm((2, 64, 256), BF), vm((2, 8, 128), F32), vm((2, 8, 128), jnp.int32),
            pltpu.SMEM((8, 128), jnp.int32),
            vm((2 * OWN + 1, 16, 128), BF), vm((OWN, 16, 128), BF), vm((np_, 32, 128), BF), vm((OWN * 32, 512), BF),
            dma((4,)), dma((4,)), dma((2,)), dma((4,)), dma((4,)), dma((3,)), dma((3,)),
            dma((K,)), dma((K,)), dma((2,)), dma((2,)), dma((2,)), dma((2,)), dma((1,)),
            dma((1,)), dma((1,)),
        ],
        compiler_params=pltpu.CompilerParams(
            vmem_limit_bytes=62 << 20, collective_id=0, has_side_effects=True),
        name="cheb",
    )(features, offsets, edge_weights, mix.transpose(0, 2, 1), bias.reshape(1, -1), owners.reshape(1, -1))
    got = got.reshape(np_, 16, 2, 128).transpose(0, 2, 1, 3).reshape(np_, 2, 2048)
    return got[None]


def solution(mesh):
    return jax.shard_map(
        body,
        mesh=mesh,
        in_specs=(
            P("chan", "patch"),
            P(None, "patch"),
            P(None, "patch"),
            P(None, None, "chan"),
            P("chan"),
            P("patch", None),
        ),
        out_specs=P("patch", None, None, "chan"),
        check_vma=False,
    )
```

```python
import functools

import jax
import jax.numpy as jnp
from jax import lax
from jax.experimental import pallas as pl
from jax.experimental.pallas import tpu as pltpu
from jax.sharding import PartitionSpec as P

MESH = pl.DeviceIdType.MESH
BF = jnp.bfloat16
F32 = jnp.float32
K = 8
CH = 64
OWN = 16
EXT = 5
NB = OWN + EXT
HALO = 640
LANES = HALO + NB * 256 + HALO
OUT_W = EXT * 256 + HALO
WIN = 1280
NPX = NB * 256
MID = 1152


def place(line):
    n, q = line // 4, line % 4
    return 2 * n + q % 2, (q // 2 + n % 2) % 2


def iota(shape, dim):
    return lax.broadcasted_iota(jnp.int32, shape, dim)


def cheb_kernel(np_, feat, offs, wts, mix, bias, own_ref, out_ref,
                tb0, tb1, tb2, tb3, tb4, tb5, tb6, fp0, fp1,
                wm, ot, wt, cor, s16, w16, mixall, biasall, inv, inv_s,
                msg, snd, outg, plhs, t0_s, t0_r, tab_l, tab_s, tab_r, par_s, par_r,
                in_s, in_r, mid_s, mid_r, sw_s, sw_r, loc, all_s, all_r):
    tb = (tb0, tb1, tb2, tb3, tb4, tb5, tb6)
    fp = (fp0, fp1)
    p = lax.axis_index("patch")
    g = lax.axis_index("chan")
    n, c = p // 2, p % 2
    gx = (g + n) % 2
    line = 4 * n + 2 * gx + c
    last = 2 * np_ - 1
    sib = (p + 1 - 2 * c, g)
    partner = (p, 1 - g)
    first_core = c == 0
    home = gx == c
    ng = np_ // 2

    outer = pl.multiple_of((1 - c) * 0 + c * (LANES - OUT_W), 128)
    for k in (3, 5):
        tb[k][:, pl.ds(outer, OUT_W)] = jnp.zeros((CH, OUT_W), BF)
    at_end = (line == 0) | (line == last)

    @pl.when(at_end)
    def _():
        tb0[:, pl.ds(outer, OUT_W)] = jnp.zeros((CH, OUT_W), BF)
        to = pl.multiple_of(c * OWN * 256, 128)
        ot[:, pl.ds(to, EXT * 256)] = jnp.zeros((8, EXT * 256), jnp.int32)
        wt[:, pl.ds(to, EXT * 256)] = jnp.zeros((8, EXT * 256), F32)

    msg[2 * OWN] = jnp.zeros((16, 128), BF)

    bar = pltpu.get_barrier_semaphore()
    for dn in (-1, 0, 1):
        for dc in (0, 1):
            for dg in (0, 1):
                pp = 2 * (n + dn) + dc

                @pl.when((n + dn >= 0) & (n + dn < ng) & ~((pp == p) & (dg == g)))
                def _():
                    pl.semaphore_signal(bar, inc=1, device_id=(pp, dg), device_id_type=MESH)

    def hello(i, carry):
        j = (i + p) % np_
        pp, gg = 2 * (j // 2) + g, j % 2

        @pl.when(~((pp == p) & (gg == g)))
        def _():
            pl.semaphore_signal(bar, inc=1, device_id=(pp, gg), device_id_type=MESH)
        return carry

    lax.fori_loop(0, np_, hello, 0)
    pl.semaphore_wait(bar, 11 - 4 * jnp.where((n == 0) | (n == ng - 1), 1, 0) + np_ - jnp.where(c == g, 1, 0))

    half = 4096
    main_dst = pl.multiple_of((1 - c) * EXT * 256, 128)
    ext_dst = pl.multiple_of(c * OWN * 256, 128)
    sib_dst = pl.multiple_of(c * EXT * 256, 128)

    def tables(fn):
        fn(0, offs, ot)
        fn(1, wts, wt)

    def tab_main_local(i, src, dst):
        return pltpu.make_async_copy(src.at[:, pl.ds(pl.multiple_of(c * half, 128), half)],
                                     dst.at[:, pl.ds(main_dst, half)], tab_l.at[i])

    def tab_main_remote(i, src, dst):
        return pltpu.make_async_remote_copy(
            src_ref=src.at[:, pl.ds(pl.multiple_of((1 - c) * half, 128), half)],
            dst_ref=dst.at[:, pl.ds(sib_dst, half)],
            send_sem=tab_s.at[i], recv_sem=tab_r.at[i], device_id=sib, device_id_type=MESH)

    def tab_ext_local(i, src, dst):
        return pltpu.make_async_copy(
            src.at[:, pl.ds(pl.multiple_of((1 - c) * (8192 - EXT * 256), 128), EXT * 256)],
            dst.at[:, pl.ds(ext_dst, EXT * 256)], tab_l.at[i])

    out_line = line - 1 + 2 * c
    outp, outg_ = place(out_line)
    has_out = ~at_end
    other_ext = pl.multiple_of((1 - c) * OWN * 256, 128)

    def tab_ext_remote(i, src, dst):
        return pltpu.make_async_remote_copy(
            src_ref=src.at[:, pl.ds(pl.multiple_of(c * (8192 - EXT * 256), 128), EXT * 256)],
            dst_ref=dst.at[:, pl.ds(other_ext, EXT * 256)],
            send_sem=tab_s.at[2 + i], recv_sem=tab_r.at[2 + i],
            device_id=(outp, outg_), device_id_type=MESH)

    @pl.when(home)
    def _():
        tables(lambda i, s, d: tab_main_local(i, s, d).start())
        tables(lambda i, s, d: tab_main_remote(i, s, d).start())

    @pl.when(~home)
    def _():
        tables(lambda i, s, d: tab_ext_local(i, s, d).start())

    row = pl.multiple_of(32 * g, 32)
    flows = (
        (2 * p, 0, HALO + 4096, LANES - HALO - 4096, 0),
        (2 * p + 1, 4096 - HALO, HALO + 4096, 0, 0),
        (2 * p - 1, 0, OUT_W, LANES - OUT_W, 2),
        (2 * p + 2, 8192 - OUT_W, OUT_W, 0, 2),
    )

    def flow_parts(i):
        target, src0, size, dst0, sem = flows[i]
        src = feat.at[:, pl.ds(src0, size)]
        dst = tb0.at[pl.ds(row, 32), pl.ds(dst0, size)]
        return target, src, dst, sem + g

    def flow_ok(i):
        target = flows[i][0]
        return (target >= 0) & (target <= last)

    def flow_remote(i):
        target, src, dst, sem = flow_parts(i)
        tp, tg = place(target)
        return pltpu.make_async_remote_copy(
            src_ref=src, dst_ref=dst, send_sem=t0_s.at[i], recv_sem=t0_r.at[sem],
            device_id=(tp, tg), device_id_type=MESH)

    def start_flows(which):
        for i in which:
            target, src, dst, sem = flow_parts(i)

            @pl.when(flow_ok(i) & (target == line))
            def _():
                pltpu.make_async_copy(src, dst, t0_r.at[sem]).start()

            @pl.when(flow_ok(i) & (target != line))
            def _():
                flow_remote(i).start()

    start_flows((0, 1))

    @pl.when(home & has_out)
    def _():
        tables(lambda i, s, d: tab_ext_remote(i, s, d).start())

    for k in (1, 2, 4, 6):
        tb[k][:, pl.ds(outer, OUT_W)] = jnp.zeros((CH, OUT_W), BF)

    mixcat = jnp.concatenate([mix[k] for k in range(K)], axis=0)
    oi, oo = iota((64, 64), 0), iota((64, 64), 1)
    wanted = (oi // 16 % 2) * 32 + 2 * (oi % 16) + oi // 32
    perm = jnp.where(oo == wanted, 1.0, 0.0).astype(BF)
    mixall[g] = lax.dot_general(perm, mixcat, (((1,), (1,)), ((), ())),
                                preferred_element_type=F32).astype(BF)
    biasall[g] = jnp.zeros((8, 128), F32)
    biasall[g, 0:1, 0:32] = bias[...]

    rowv = jnp.broadcast_to(own_ref[...], (32, 32))
    si, sl = iota((32, 32), 0), iota((32, 32), 1)
    bi, bl = iota((32, 128), 0), iota((32, 128), 1)
    col = jnp.sum(jnp.where(si == sl, rowv, 0), axis=1, keepdims=True)
    same = (jnp.broadcast_to(col, (32, 32)) == rowv) & (sl < si)
    slot = jnp.sum(jnp.where(same, 1, 0), axis=1, keepdims=True)
    key = col * 2 + slot
    hit = jnp.sum(jnp.where(jnp.broadcast_to(key, (32, 128)) == bl, bi + 1, 0), axis=0, keepdims=True)
    inv[c] = jnp.broadcast_to(jnp.where(hit == 0, 2 * OWN, hit - 1), (8, 128))

    par = [
        pltpu.make_async_remote_copy(src_ref=mixall.at[g], dst_ref=mixall.at[g], send_sem=par_s.at[0],
                                     recv_sem=par_r.at[0], device_id=partner, device_id_type=MESH),
        pltpu.make_async_remote_copy(src_ref=biasall.at[g], dst_ref=biasall.at[g], send_sem=par_s.at[1],
                                     recv_sem=par_r.at[1], device_id=partner, device_id_type=MESH),
        pltpu.make_async_remote_copy(src_ref=inv.at[c], dst_ref=inv.at[c], send_sem=par_s.at[2],
                                     recv_sem=par_r.at[2], device_id=sib, device_id_type=MESH),
    ]
    for cp in par:
        cp.start()

    def block_of(i):
        return c * i + (1 - c) * (NB - 1 - i)

    base = [(iota((16, 128), 0) + 16 * r).astype(jnp.int16) for r in range(16)]

    def build(i, carry):
        b = block_of(i)
        lanes = pl.ds(pl.multiple_of(256 * b, 256), 256)
        s = iota((8, 256), 1) + ot[:, lanes] + 512
        w = wt[:, lanes]
        cl = jnp.sum(jnp.where(s == -1, w, 0.0), axis=0, keepdims=True)
        cr = jnp.sum(jnp.where(s == WIN, w, 0.0), axis=0, keepdims=True)
        cor[b, 0:1, :] = cl
        cor[b, 1:2, :] = cr
        full = w
        for r in range(1, 8):
            full = full + jnp.where(s == pltpu.roll(s, r, 0), pltpu.roll(w, r, 0), 0.0)
        for j in range(8):
            s16[j] = jnp.broadcast_to(s[j:j + 1], (16, 256)).astype(jnp.int16)
            w16[j] = jnp.broadcast_to(full[j:j + 1], (16, 256)).astype(BF)
        for h in range(2):
            px = slice(128 * h, 128 * h + 128)
            first, stop = (0, 73) if h == 0 else (7, 80)
            wm[b, slice(16 * stop, WIN) if h == 0 else slice(0, 16 * first), px] = jnp.zeros((112, 128), BF)
            for q in range(first, stop, 16):
                rows = range(min(16, stop - q))
                acc = [jnp.zeros((16, 128), BF) for r in rows]
                for j in range(8):
                    sq = s16[j, :, px] - jnp.int16(16 * q)
                    wq = w16[j, :, px]
                    acc = [jnp.where(base[r] == sq, wq, acc[r]) for r in rows]
                for r in rows:
                    wm[b, 16 * (q + r):16 * (q + r + 1), px] = acc[r]
        return carry

    lo1 = jnp.where(home, 0, OWN)
    hi1 = jnp.where(home, OWN, NB)
    lo2 = jnp.where(home, OWN, 0)
    hi2 = jnp.where(home, NB, OWN)

    @pl.when(home)
    def _():
        tables(lambda i, s, d: tab_main_local(i, s, d).wait())

    @pl.when(~home)
    def _():
        tables(lambda i, s, d: tab_ext_local(i, s, d).wait())

    lax.fori_loop(lo1, lo1 + 5, build, 0)
    start_flows((2, 3))
    lax.fori_loop(lo1 + 5, hi1, build, 0)

    @pl.when(~home)
    def _():
        tables(lambda i, s, d: pltpu.make_async_copy(
            s.at[:, pl.ds(0, half)], d.at[:, pl.ds(main_dst, half)], tab_r.at[i]).wait())

    @pl.when(home & has_out)
    def _():
        tables(lambda i, s, d: pltpu.make_async_copy(
            s.at[:, pl.ds(0, EXT * 256)], d.at[:, pl.ds(ext_dst, EXT * 256)], tab_r.at[2 + i]).wait())

    lax.fori_loop(lo2, hi2, build, 0)

    main_at = pl.multiple_of((1 - c) * (LANES - HALO - 4096), 128)
    for gg in range(2):
        pltpu.make_async_copy(feat.at[:, pl.ds(0, HALO + 4096)],
                              tb0.at[pl.ds(32 * gg, 32), pl.ds(main_at, HALO + 4096)],
                              t0_r.at[gg]).wait()

    def term(k, i):
        b = block_of(i)
        at = pl.multiple_of(256 * b, 256)
        src = tb[k - 1]
        win = src[:, pl.ds(at + 128, WIN)]
        left = pltpu.roll(src[:, pl.ds(at, 128)].astype(F32), 1, 1)
        right = pltpu.roll(src[:, pl.ds(at + 1408, 128)].astype(F32), 127, 1)
        u0 = jnp.dot(win, wm[b, :, 0:128], preferred_element_type=F32) + left * cor[b, 0:1, 0:128]
        u1 = jnp.dot(win, wm[b, :, 128:256], preferred_element_type=F32) + right * cor[b, 1:2, 128:256]
        u = jnp.concatenate([u0, u1], axis=1)
        if k == 1:
            t = u
        elif k == 2:
            t = 2.0 * u - tb0[:, pl.ds(at + HALO, 256)].astype(F32)
        else:
            t = 2.0 * u - fp[k % 2][:, pl.ds(at, 256)]
        return at, t

    def run(k, lo, hi, group=10):
        def one(i):
            at, t = term(k, i)
            fp[k % 2][:, pl.ds(at, 256)] = t
            tb[k][:, pl.ds(at + HALO, 256)] = t.astype(BF)

        full = (hi - lo) // group

        def some(m, carry):
            for r in range(group):
                one(lo + m * group + r)
            return carry

        first = lo
        if full > 1:
            lax.fori_loop(0, full, some, 0)
            first = lo + full * group
        for i in range(first, hi):
            one(i)

    own_at = HALO + (1 - c) * EXT * 256
    edge_src = pl.multiple_of(own_at + (1 - c) * (4096 - HALO), 128)
    edge_dst = pl.multiple_of(c * (LANES - HALO), 128)

    def inner(k):
        return pltpu.make_async_remote_copy(
            src_ref=tb[k].at[:, pl.ds(edge_src, HALO)], dst_ref=tb[k].at[:, pl.ds(edge_dst, HALO)],
            send_sem=in_s.at[k], recv_sem=in_r.at[k], device_id=sib, device_id_type=MESH)

    def mid(k):
        src = pl.multiple_of(own_at + c * (4096 - MID), 128)
        dst = pl.multiple_of((1 - c) * (LANES - OUT_W) + c * (OUT_W - MID), 128)
        return pltpu.make_async_remote_copy(
            src_ref=tb[k].at[:, pl.ds(src, MID)], dst_ref=tb[k].at[:, pl.ds(dst, MID)],
            send_sem=mid_s.at[k // 4], recv_sem=mid_r.at[k // 4], device_id=(outp, outg_), device_id_type=MESH)

    run(1, 0, 3)
    inner(1).start()
    run(1, 3, 13)

    @pl.when(has_out)
    def _():
        for gg in range(2):
            pltpu.make_async_copy(feat.at[:, pl.ds(0, OUT_W)],
                                  tb0.at[pl.ds(32 * gg, 32), pl.ds(outer, OUT_W)],
                                  t0_r.at[2 + gg]).wait()

    run(1, 13, NB)
    inner(1).wait_recv()
    run(2, 0, 3)
    inner(2).start()
    run(2, 3, 19)
    inner(2).wait_recv()
    run(3, 11, 16)

    @pl.when(has_out)
    def _():
        mid(3).start()

    pltpu.make_async_copy(mixall.at[1 - g], mixall.at[1 - g], par_r.at[0]).wait()
    pltpu.make_async_copy(biasall.at[1 - g], biasall.at[1 - g], par_r.at[1]).wait()
    pltpu.make_async_copy(inv.at[1 - c], inv.at[1 - c], par_r.at[2]).wait()
    to_smem = pltpu.make_async_copy(inv.at[gx], inv_s, loc.at[0])
    to_smem.start()
    o1, l1 = iota((64, 128), 0), iota((64, 128), 1)
    brow = jnp.where(o1 // 16 % 2 == 0, biasall[0, 0:1, :], biasall[1, 0:1, :])
    bcol = jnp.sum(jnp.where(l1 == 2 * (o1 % 16) + o1 // 32, brow, 0.0), axis=1, keepdims=True)
    pi, pq = iota((512, 128), 0), iota((512, 128), 1)
    pool = jnp.where(pi % 256 // 4 + 64 * (pi // 256) == pq, 0.25, 0.0).astype(BF)
    to_smem.wait()

    run(3, 0, 3)
    inner(3).start()
    run(3, 3, 11)
    inner(3).wait_recv()
    run(4, 0, 3)
    inner(4).start()
    run(4, 3, 13)
    inner(4).wait_recv()
    run(5, 0, 3)
    inner(5).start()
    run(5, 3, 10)
    inner(5).wait_recv()
    run(6, 0, 3)
    inner(6).start()

    @pl.when(has_out)
    def _():
        mid(3).wait_recv()

    run(4, 13, 19)
    run(5, 10, 16)

    @pl.when(has_out)
    def _():
        mid(5).start()

    run(6, 3, 13)
    inner(6).wait_recv()

    def finish(i):
        at, t = term(7, i)
        t = t.astype(BF)
        total = bcol
        for gg in range(2):
            rows = slice(32 * gg, 32 * gg + 32)
            rhs = jnp.concatenate([tb[k][rows, pl.ds(at + HALO, 256)] for k in range(K - 1)] + [t[rows]], axis=0)
            part = jnp.dot(mixall[gg], rhs, preferred_element_type=F32)
            total = total + part.astype(BF).astype(F32)
        filt = jnp.maximum(total, 0.0).astype(BF)
        plhs[32 * i:32 * i + 32, 0:256] = filt[0:32]
        plhs[32 * i:32 * i + 32, 256:512] = filt[32:64]

    def pool_blocks(m):
        pooled = jnp.dot(plhs[256 * m:256 * m + 256, :], pool, preferred_element_type=F32)
        for r in range(8):
            b = block_of(8 * m + r) - (1 - c) * EXT
            even, odd = pooled[32 * r:32 * r + 16], pooled[32 * r + 16:32 * r + 32]
            msg[c * OWN + b] = jnp.where(c == 0, even, odd).astype(BF)
            snd[b] = jnp.where(c == 0, odd, even).astype(BF)

    def swap(m):
        b0 = c * 8 * m + (1 - c) * (8 - 8 * m)
        return pltpu.make_async_remote_copy(
            src_ref=snd.at[pl.ds(b0, 8)], dst_ref=msg.at[pl.ds(c * OWN + b0, 8)],
            send_sem=sw_s.at[m], recv_sem=sw_r.at[m], device_id=sib, device_id_type=MESH)

    for i in range(0, 8):
        finish(i)
    pool_blocks(0)
    swap(0).start()
    for i in range(8, 10):
        finish(i)

    @pl.when(has_out)
    def _():
        mid(5).wait_recv()

    run(6, 13, 19)
    for i in range(10, 16):
        finish(i)
    pool_blocks(1)
    swap(1).start()
    for m in range(2):
        pltpu.make_async_copy(msg.at[pl.ds((1 - c) * OWN + 8 * m, 8)],
                              msg.at[pl.ds((1 - c) * OWN + 8 * m, 8)], sw_r.at[m]).wait()

    ei, ej = iota((32, 32), 0), iota((32, 32), 1)
    weave = jnp.where(ej == (ei % 2) * 16 + ei // 2, 1.0, 0.0).astype(BF)
    src_patch = 2 * n + gx

    def assemble(i, carry):
        m = (i + p // 4) % (np_ // 4)
        cols = []
        for r in range(4):
            o = 4 * m + r
            cols.append(jnp.concatenate([msg[inv_s[0, 2 * o]], msg[inv_s[0, 2 * o + 1]]], axis=0))
        res = jnp.dot(weave, jnp.concatenate(cols, axis=1), preferred_element_type=F32).astype(BF)
        for r in range(4):
            outg[4 * m + r] = res[:, 128 * r:128 * (r + 1)]
        for r in range(4):
            o = 4 * m + r
            me = (o == p) & (c == g)

            @pl.when(me)
            def _():
                pltpu.make_async_copy(outg.at[o], out_ref.at[src_patch], all_r.at[0]).start()

            @pl.when(~me)
            def _():
                pltpu.make_async_remote_copy(
                    src_ref=outg.at[o], dst_ref=out_ref.at[src_patch], send_sem=all_s.at[0],
                    recv_sem=all_r.at[0], device_id=(o, c), device_id_type=MESH).start()
        return carry

    lax.fori_loop(0, np_ // 4, assemble, 0)

    @pl.when(home)
    def _():
        tables(lambda i, s, d: tab_main_remote(i, s, d).wait_send())

    @pl.when(home & has_out)
    def _():
        tables(lambda i, s, d: tab_ext_remote(i, s, d).wait_send())

    for i in range(4):
        @pl.when(flow_ok(i) & (flows[i][0] != line))
        def _():
            flow_remote(i).wait_send()

    for cp in par:
        cp.wait_send()
    for k in range(1, K - 1):
        inner(k).wait_send()

    @pl.when(has_out)
    def _():
        mid(3).wait_send()
        mid(5).wait_send()

    for m in range(2):
        swap(m).wait_send()

    pltpu.make_async_copy(out_ref.at[:], out_ref.at[:], all_r.at[0]).wait()
    pltpu.make_async_copy(outg.at[pl.ds(0, np_ - 1)], outg.at[pl.ds(0, np_ - 1)], all_s.at[0]).wait()

    @pl.when(c != g)
    def _():
        pltpu.make_async_copy(outg.at[0], outg.at[0], all_s.at[0]).wait()


def copy_kernel(src, dst, buf, sa, sb):
    step = src.shape[0] // 8

    def part(ref, i):
        return ref.at[pl.ds(i * step, step)]

    ins = [pltpu.make_async_copy(part(src, i), part(buf, i), sa.at[i]) for i in range(8)]
    outs = [pltpu.make_async_copy(part(buf, i), part(dst, i), sb.at[i]) for i in range(8)]
    for cp in ins:
        cp.start()
    for i in range(8):
        ins[i].wait()
        outs[i].start()
    for cp in outs:
        cp.wait()


def body(features, offsets, edge_weights, mix, bias, owners):
    np_ = lax.axis_size("patch")
    any_, vmem = pl.BlockSpec(memory_space=pl.ANY), pl.BlockSpec(memory_space=pltpu.VMEM)
    dma, vm = pltpu.SemaphoreType.DMA, pltpu.VMEM
    got = pl.pallas_call(
        functools.partial(cheb_kernel, np_),
        out_shape=jax.ShapeDtypeStruct((np_, 32, 128), BF),
        in_specs=[any_, any_, any_, vmem, vmem, vmem],
        out_specs=any_,
        scratch_shapes=[
            *[vm((CH, LANES), BF)] * (K - 1), *[vm((CH, NPX), F32)] * 2, vm((NB, WIN, 256), BF),
            vm((8, NPX), jnp.int32), vm((8, NPX), F32), vm((NB, 8, 256), F32),
            vm((8, 16, 256), jnp.int16), vm((8, 16, 256), BF),
            vm((2, 64, 256), BF), vm((2, 8, 128), F32), vm((2, 8, 128), jnp.int32),
            pltpu.SMEM((8, 128), jnp.int32),
            vm((2 * OWN + 1, 16, 128), BF), vm((OWN, 16, 128), BF), vm((np_, 32, 128), BF), vm((OWN * 32, 512), BF),
            dma((4,)), dma((4,)), dma((2,)), dma((4,)), dma((4,)), dma((3,)), dma((3,)),
            dma((K,)), dma((K,)), dma((2,)), dma((2,)), dma((2,)), dma((2,)), dma((1,)),
            dma((1,)), dma((1,)),
        ],
        compiler_params=pltpu.CompilerParams(
            vmem_limit_bytes=62 << 20, collective_id=0, has_side_effects=True),
        name="cheb",
    )(features, offsets, edge_weights, mix.transpose(0, 2, 1), bias.reshape(1, -1), owners.reshape(1, -1))
    got = pl.pallas_call(
        copy_kernel,
        out_shape=jax.ShapeDtypeStruct((np_, 32, 128), BF),
        in_specs=[any_],
        out_specs=any_,
        scratch_shapes=[vm((np_, 32, 128), BF), dma((8,)), dma((8,))],
        compiler_params=pltpu.CompilerParams(vmem_limit_bytes=62 << 20),
        name="keep",
    )(got)
    got = got.reshape(np_, 16, 2, 128).transpose(0, 2, 1, 3).reshape(np_, 2, 2048)
    return got[None]


def solution(mesh):
    return jax.shard_map(
        body,
        mesh=mesh,
        in_specs=(
            P("chan", "patch"),
            P(None, "patch"),
            P(None, "patch"),
            P(None, None, "chan"),
            P("chan"),
            P("patch", None),
        ),
        out_specs=P("patch", None, None, "chan"),
        check_vma=False,
    )
```
